32 devices in a mesh: seq: 4 (over y, core), batch: 8 (over z, x).
Axes of the slice: x: 2, y: 2, z: 4, core: 2. Of those that a mesh axis runs over, the one named last changes fastest.
Arguments:
- hidden: bfloat16 [8, 1536, 1024], P('batch', 'seq'), may hold values from -6 to 6
- grad_out: bfloat16 [8, 1536, 1024], P('batch', 'seq'), may hold values from -6 to 6
- block_offsets: int32 [8, 16, 12, 4], P('batch', 'seq'), may hold values from 0 to 11, as said below
- w_query: bfloat16 [1024, 1024], replicated, may hold values from -0.1875 to 0.1875
- w_key: bfloat16 [1024, 1024], replicated, may hold values from -0.1875 to 0.1875
- w_value: bfloat16 [1024, 1024], replicated, may hold values from -0.1875 to 0.1875
- w_out: bfloat16 [1024, 1024], replicated, may hold values from -0.1875 to 0.1875
Outputs:
- grad_hidden: bfloat16 [8, 1536, 1024], P('batch', 'seq')
- grad_weights: float32 [4, 1024, 1024], P(None, 'batch', 'seq')
The draws below stay inside these ranges and needn't reach their ends.
Inputs may be any that keep to these rules, and one draw needn't show every extreme that they name: `block_offsets`: slot 0 of every list is 0 (the query's own block); the other slots of a list hold distinct values from 1 to 11, and a value greater than the query block's index leaves its slot empty.
All inputs are finite; a program needn't handle non-finite values.
Results may differ from the reference program's by a relative error of at most 0.012.
Values may be sent and summed in bfloat16 or wider, within the bound.
No kernel may reach another device: no remote copies, remote signals or barrier semaphores. Data moves between devices by JAX's collectives and lax.ppermute only.
A program may use at most 128 MiB of HBM per device.

```python
import math
import jax
import jax.numpy as jnp
from jax import lax

D = 1024
H = 16
HD = 64
BLK = 128
NSEL = 4
SEQ_LEN = 1536
QB = 12
NCHUNK = 8


def draw_hidden(key, part):
    base = jax.random.normal(jax.random.fold_in(key, 11), (NCHUNK, SEQ_LEN, D), jnp.float32)
    base = jnp.clip(base, -6.0, 6.0)
    return base.astype(jnp.bfloat16)


def draw_block_offsets(key, part):
    ranks = jax.random.randint(jax.random.fold_in(key, 21), (NCHUNK, H, QB, QB - 1), 0, 1 << 20, dtype=jnp.int32)
    ranks = ranks * (QB - 1) + jnp.arange(QB - 1, dtype=jnp.int32)
    order = jnp.argsort(ranks, axis=-1, stable=True)[..., :NSEL - 1].astype(jnp.int32) + 1
    own_block = jnp.zeros((NCHUNK, H, QB, 1), jnp.int32)
    return jnp.concatenate([own_block, order], axis=-1)


def steps_of(stream_key, dims, cuts, smallest, largest):
    gain, own = 1.0, jax.random.fold_in(stream_key, 6)
    for axis_at, blocks in cuts:
        heights = jnp.exp(jax.random.uniform(jax.random.fold_in(own, axis_at), (blocks,), jnp.float32, smallest / len(cuts), largest / len(cuts)))
        gain = gain * jnp.repeat(heights, dims[axis_at] // blocks).reshape([-1 if axis == axis_at else 1 for axis in range(len(dims))])
    return gain


def noise(stream_key, dims, deviation, reach, split=(), held_as=jnp.bfloat16):
    gain = steps_of(stream_key, dims, split, -0.22, 0.18) if split else 1.0
    result = jax.random.normal(stream_key, dims, jnp.float32) * deviation * gain
    return jnp.minimum(jnp.maximum(result, -reach), reach).astype(held_as)


def setup_inputs(seed: int = 0) -> dict:
    key_list = jax.random.split(jax.random.key(seed), 8)
    hidden = draw_hidden(jax.random.fold_in(key_list[7], 71), 0)
    grad_out = noise(key_list[1], (NCHUNK, SEQ_LEN, D), 1.0, 6.0, ((0, 8), (1, 4)))
    block_offsets = draw_block_offsets(jax.random.fold_in(key_list[7], 71), 0)
    w_query = noise(key_list[3], (D, D), D ** -0.5, 0.1875)
    w_key = noise(key_list[4], (D, D), D ** -0.5, 0.1875)
    w_value = noise(key_list[5], (D, D), D ** -0.5, 0.1875)
    w_out = noise(key_list[6], (D, D), D ** -0.5, 0.1875)
    return dict(hidden=hidden, grad_out=grad_out, block_offsets=block_offsets, w_query=w_query, w_key=w_key, w_value=w_value, w_out=w_out)


def pick_blocks(source, chosen):
    return source[chosen]

def add_blocks(running, chosen, portion):
    return running.at[chosen].add(portion)

def scatter_blocks(running, block_ids, portion):
    heads_n = portion.shape[0]
    flat_ids = block_ids.reshape(heads_n, -1)
    flat_part = portion.reshape((heads_n, -1) + portion.shape[3:])
    return jax.vmap(add_blocks)(running, flat_ids, flat_part)

def attend_group(queries, key_all, value_all, out_grads, offsets, first_block):
    group_len = queries.shape[1]
    block_len = queries.shape[2]
    score_scale = 1.0 / math.sqrt(queries.shape[3])
    query_block = first_block + jnp.arange(group_len, dtype=jnp.int32)
    usable = offsets <= query_block[None, :, None]
    block_ids = jnp.where(usable, query_block[None, :, None] - offsets, 0).astype(jnp.int32)
    picked_keys = jax.vmap(pick_blocks)(key_all, block_ids)
    picked_values = jax.vmap(pick_blocks)(value_all, block_ids)
    scores = jnp.einsum('hgqd,hgnkd->hgqnk', queries.astype(jnp.float32), picked_keys.astype(jnp.float32)) * score_scale
    within = jnp.arange(block_len, dtype=jnp.int32)
    query_pos = query_block[:, None] * block_len + within[None, :]
    key_pos = block_ids[..., None] * block_len + within
    allowed = usable[:, :, None, :, None] & (key_pos[:, :, None, :, :] <= query_pos[None, :, :, None, None])
    row_top = lax.optimization_barrier(jnp.max(jnp.where(allowed, scores, -jnp.inf), axis=(3, 4), keepdims=True))
    raised = jnp.where(allowed, jnp.exp(scores - row_top), 0.0)
    denom_sum = lax.optimization_barrier(jnp.sum(raised, axis=(3, 4), keepdims=True))
    probabilities = raised / denom_sum
    probs_half = probabilities.astype(jnp.bfloat16)
    attended = jnp.einsum('hgqnk,hgnkd->hgqd', probs_half.astype(jnp.float32), picked_values.astype(jnp.float32)).astype(jnp.bfloat16)
    delta_rows = lax.optimization_barrier(jnp.sum(out_grads.astype(jnp.float32) * attended.astype(jnp.float32), axis=-1))
    prob_grad = jnp.einsum('hgqd,hgnkd->hgqnk', out_grads.astype(jnp.float32), picked_values.astype(jnp.float32))
    score_grad = (probabilities * (prob_grad - delta_rows[:, :, :, None, None])).astype(jnp.bfloat16)
    query_grad = (jnp.einsum('hgqnk,hgnkd->hgqd', score_grad.astype(jnp.float32), picked_keys.astype(jnp.float32)) * score_scale).astype(jnp.bfloat16)
    key_part = jnp.einsum('hgqnk,hgqd->hgnkd', score_grad.astype(jnp.float32), queries.astype(jnp.float32)) * score_scale
    value_part = jnp.einsum('hgqnk,hgqd->hgnkd', probs_half.astype(jnp.float32), out_grads.astype(jnp.float32))
    return (attended, query_grad, key_part, value_part, block_ids)

def heads_first(matrix):
    return matrix.reshape(QB, BLK, H, HD).transpose(2, 0, 1, 3)

def tokens_first(blocks):
    return blocks.transpose(1, 2, 0, 3).reshape(SEQ_LEN, H * HD)

def reference(hidden, grad_out, block_offsets, w_query, w_key, w_value, w_out):

    def one_stretch(running, inputs):
        tokens, grad_rows, offsets = inputs
        queries = jnp.dot(tokens, w_query, preferred_element_type=jnp.float32).astype(jnp.bfloat16)
        key_rows = jnp.dot(tokens, w_key, preferred_element_type=jnp.float32).astype(jnp.bfloat16)
        value_rows = jnp.dot(tokens, w_value, preferred_element_type=jnp.float32).astype(jnp.bfloat16)
        attn_grad = jnp.dot(grad_rows, w_out.T, preferred_element_type=jnp.float32).astype(jnp.bfloat16)
        attended, query_grad, key_part, value_part, block_ids = attend_group(heads_first(queries), heads_first(key_rows), heads_first(value_rows), heads_first(attn_grad), offsets, jnp.int32(0))
        empty = jnp.zeros((H, QB, BLK, HD), jnp.float32)
        key_grad = scatter_blocks(empty, block_ids, key_part).astype(jnp.bfloat16)
        value_grad = scatter_blocks(empty, block_ids, value_part).astype(jnp.bfloat16)
        query_tok = tokens_first(query_grad)
        key_tok = tokens_first(key_grad)
        value_tok = tokens_first(value_grad)
        attended_tok = tokens_first(attended)
        grad_hidden = (jnp.dot(query_tok, w_query.T, preferred_element_type=jnp.float32) + jnp.dot(key_tok, w_key.T, preferred_element_type=jnp.float32) + jnp.dot(value_tok, w_value.T, preferred_element_type=jnp.float32)).astype(jnp.bfloat16)
        term_rows = jnp.stack([jnp.dot(tokens.T, query_tok, preferred_element_type=jnp.float32), jnp.dot(tokens.T, key_tok, preferred_element_type=jnp.float32), jnp.dot(tokens.T, value_tok, preferred_element_type=jnp.float32), jnp.dot(attended_tok.T, grad_rows, preferred_element_type=jnp.float32)])
        return (running + term_rows, grad_hidden)
    summed, grad_hidden = lax.scan(one_stretch, jnp.zeros((4, D, D), jnp.float32), (hidden, grad_out, block_offsets))
    return (grad_hidden, summed * (1.0 / math.sqrt(NCHUNK * SEQ_LEN)))
```

```python
import functools
import math

import jax
import jax.numpy as jnp
from jax import lax
from jax.experimental import pallas as pl
from jax.experimental.pallas import tpu as pltpu
from jax.sharding import PartitionSpec as P

BLK = 128
BF = jnp.bfloat16
F32 = jnp.float32
LAST_LAST = (((1,), (1,)), ((), ()))
FIRST_LAST = (((0,), (1,)), ((), ()))
FIRST_FIRST = (((0,), (0,)), ((), ()))


def dot(left_side, right_side, dims):
    return lax.dot_general(left_side, right_side, dims, preferred_element_type=F32)


def swap(value, axis, distance):
    count = lax.axis_size(axis)
    return lax.ppermute(value, axis, [(at, at ^ distance) for at in range(count)])


def gather_pieces(shard, axis):
    pieces = {0: shard}
    bit = lax.axis_size(axis) // 2
    while bit:
        for place in sorted(pieces):
            pieces[place | bit] = swap(pieces[place], axis, bit)
        bit //= 2
    return [pieces[place] for place in sorted(pieces)]


def attention_kernel(
    place_of,
    offsets,
    queries_t,
    out_grads_t,
    keys_t,
    values_t,
    keys,
    values,
    attended_t,
    query_grad_t,
    key_grad_t,
    value_grad_t,
    key_acc,
    value_acc,
    *,
    blocks,
    slots,
    head_size,
):
    pair = pl.program_id(0)
    key_acc[...] = jnp.zeros_like(key_acc)
    value_acc[...] = jnp.zeros_like(value_acc)
    key_at = lax.broadcasted_iota(jnp.int32, (BLK, BLK), 0)
    query_at = lax.broadcasted_iota(jnp.int32, (BLK, BLK), 1)
    causal = key_at <= query_at
    first_head = lax.broadcasted_iota(jnp.int32, (2 * head_size, BLK), 0) < head_size
    plus = functools.partial(functools.reduce, jnp.add)

    def one_block(place, carry):
        block = place_of[place]
        cols = pl.ds(pl.multiple_of(place * BLK, BLK), BLK)
        pair_queries = queries_t[:, cols]
        pair_grads = out_grads_t[:, cols]
        scored = []
        for half in range(2):
            head = 2 * pair + half
            rows = slice(half * head_size, (half + 1) * head_size)
            keep = first_head if half == 0 else ~first_head
            head_queries = jnp.where(keep, pair_queries, jnp.zeros_like(pair_queries))
            head_grads = jnp.where(keep, pair_grads, jnp.zeros_like(pair_grads))
            named, usable = [], []
            for slot in range(slots):
                offset = offsets[(head * blocks + block) * slots + slot]
                usable.append(offset <= block)
                named.append(place_of[jnp.where(offset <= block, block - offset, 0)])
            spans = [pl.ds(pl.multiple_of(at * BLK, BLK), BLK) for at in named]
            scores = [
                jnp.dot(keys[span, :], head_queries, preferred_element_type=F32) for span in spans
            ]
            prob_grad = [
                jnp.dot(values[span, :], head_grads, preferred_element_type=F32) for span in spans
            ]
            scores = [
                jnp.where(causal if slot == 0 else usable[slot], scores[slot], -jnp.inf)
                for slot in range(slots)
            ]
            scored.append((rows, named, spans, scores, prob_grad))
        parts = []
        for rows, named, spans, scores, prob_grad in scored:
            top = jnp.max(functools.reduce(jnp.maximum, scores), axis=0, keepdims=True)
            raised = [jnp.exp(part - top) for part in scores]
            total = jnp.sum(plus(raised), axis=0, keepdims=True)
            inverse = 1.0 / total
            probs = [part * inverse for part in raised]
            probs_half = [part.astype(BF) for part in probs]
            attended = plus(
                [
                    jnp.dot(values_t[rows, span], part, preferred_element_type=F32)
                    for span, part in zip(spans, probs_half)
                ]
            ).astype(BF)
            attended_t[rows, cols] = attended
            grads = out_grads_t[rows, cols]
            delta = jnp.sum(grads.astype(F32) * attended.astype(F32), axis=0, keepdims=True)
            score_grad = [
                (part * (grad - delta)).astype(BF) for part, grad in zip(probs, prob_grad)
            ]
            query_grad = plus(
                [
                    jnp.dot(keys_t[rows, span], part, preferred_element_type=F32)
                    for span, part in zip(spans, score_grad)
                ]
            )
            query_grad_t[rows, cols] = (query_grad * (1.0 / math.sqrt(head_size))).astype(BF)
            queries = queries_t[rows, cols]
            value_parts = [dot(grads, part, LAST_LAST) for part in probs_half]
            key_parts = [dot(queries, part, LAST_LAST) for part in score_grad]
            parts.append((rows, named, key_parts, value_parts))
        for rows, named, key_parts, value_parts in parts:
            for at, key_part, value_part in zip(named, key_parts, value_parts):
                key_acc[at, rows, :] += key_part
                value_acc[at, rows, :] += value_part
        return carry

    lax.fori_loop(0, blocks, one_block, 0)
    for at in range(blocks):
        span = slice(at * BLK, (at + 1) * BLK)
        key_grad_t[:, span] = key_acc[at].astype(BF)
        value_grad_t[:, span] = value_acc[at].astype(BF)


def attention(place_of, offsets, queries_t, out_grads_t, keys_t, values_t, keys, values):
    width, tokens = queries_t.shape
    heads, blocks, slots = offsets.shape
    head_size = width // heads
    pair_rows = pl.BlockSpec((2 * head_size, tokens), lambda pair, *_: (pair, 0))
    pair_cols = pl.BlockSpec((tokens, 2 * head_size), lambda pair, *_: (0, pair))
    result = jax.ShapeDtypeStruct((width, tokens), BF)
    pair_flops = 2 * 6 * BLK * BLK * head_size
    return pl.pallas_call(
        functools.partial(attention_kernel, blocks=blocks, slots=slots, head_size=head_size),
        grid_spec=pltpu.PrefetchScalarGridSpec(
            num_scalar_prefetch=2,
            grid=(heads // 2,),
            in_specs=[pair_rows] * 4 + [pair_cols] * 2,
            out_specs=[pair_rows] * 4,
            scratch_shapes=[pltpu.VMEM((blocks, 2 * head_size, BLK), F32)] * 2,
        ),
        out_shape=[result] * 4,
        compiler_params=pltpu.CompilerParams(vmem_limit_bytes=40 * 1024 * 1024),
        cost_estimate=pl.CostEstimate(
            flops=heads * blocks * slots * pair_flops,
            bytes_accessed=10 * width * tokens * 2,
            transcendentals=heads * blocks * slots * BLK * BLK,
        ),
        name="attention",
    )(place_of, offsets.reshape(-1), queries_t, out_grads_t, keys_t, values_t, keys, values)


def sum_over_batch(terms):
    count = lax.axis_size("batch")
    me = lax.axis_index("batch")
    rows, width = terms.shape
    block = width // count
    pieces = {
        place: lax.dynamic_slice(terms, (0, (me ^ place) * block), (rows, block))
        for place in range(count)
    }
    low = 1
    while low < count:
        span = 2 if low == 1 or low * 4 > count else 4
        kept = [place for place in pieces if (place // low) % span == 0]
        summed = {place: pieces[place] for place in kept}
        for step in range(1, span):
            sent = jnp.concatenate([pieces[place + step * low] for place in kept], axis=1)
            came = swap(sent.astype(BF), "batch", step * low)
            for at, place in enumerate(kept):
                summed[place] = summed[place] + came[:, at * block : (at + 1) * block].astype(F32)
        pieces = summed
        low *= span
    return pieces[0]


def rows_to_owner(block_sum):
    seq_count, batch_count = lax.axis_size("seq"), lax.axis_size("batch")
    batch_at = lax.axis_index("batch")
    ratio = batch_count // seq_count
    height, width = block_sum.shape[0] // ratio, block_sum.shape[1]
    placed = jnp.zeros((height, ratio * width), F32)
    for turn in range(ratio):
        moves = []
        for b in range(batch_count):
            for s in range(seq_count):
                target = (b // ratio) * batch_count + ratio * s + (b + turn) % ratio
                moves.append((s * batch_count + b, target))
        piece = lax.dynamic_slice(
            block_sum, (((batch_at + turn) % ratio) * height, 0), (height, width)
        )
        came = lax.ppermute(piece, ("seq", "batch"), moves)
        placed = lax.dynamic_update_slice(
            placed, came, (0, ((batch_at - turn) % ratio) * width)
        )
    return placed


def per_device(hidden, grad_out, block_offsets, w_query, w_key, w_value, w_out):
    tokens = hidden[0]
    grad_rows = grad_out[0]
    offsets = block_offsets[0]
    row_count, width = tokens.shape
    seq_count = lax.axis_size("seq")
    batch_count = lax.axis_size("batch")
    seq_at = lax.axis_index("seq")
    head_width = width // seq_count
    head_size = head_width // offsets.shape[0]

    def head_rows(weight, seq_index):
        return lax.dynamic_slice(weight, (0, seq_index * head_width), (width, head_width)).T

    def three_rows(seq_index):
        return jnp.concatenate(
            [head_rows(weight, seq_index) for weight in (w_query, w_key, w_value)], axis=0
        )

    own_rows = three_rows(seq_at)
    chip_rows = jnp.concatenate([own_rows, three_rows(seq_at ^ 1)], axis=0)
    out_rows = lax.dynamic_slice(w_out, (seq_at * head_width, 0), (head_width, width))

    hidden_all = jnp.concatenate(gather_pieces(tokens, "seq"), axis=0)
    grad_all = jnp.concatenate(gather_pieces(grad_rows, "seq"), axis=0)
    heads_t = dot(own_rows, hidden_all, LAST_LAST).astype(BF)
    out_grads_t = dot(out_rows, grad_all, LAST_LAST).astype(BF)
    queries_t = heads_t[:head_width] * jnp.asarray(1.0 / math.sqrt(head_size), BF)
    keys_t = heads_t[head_width : 2 * head_width]
    values_t = heads_t[2 * head_width :]
    keys, values = keys_t.T, values_t.T

    shard_blocks = row_count // BLK
    block_at = jnp.arange(shard_blocks * seq_count, dtype=jnp.int32)
    place_of = ((block_at // shard_blocks) ^ seq_at) * shard_blocks + block_at % shard_blocks
    attended_t, query_grad_t, key_grad_t, value_grad_t = attention(
        place_of, offsets, queries_t, out_grads_t, keys_t, values_t, keys, values
    )
    grads_t = jnp.concatenate([query_grad_t, key_grad_t, value_grad_t], axis=0)

    by_place = grads_t.reshape(3 * head_width, seq_count // 2, 2, row_count)
    came = swap(by_place[:, :, 1], "seq", 1)
    chip_grads = jnp.concatenate([by_place[:, :, 0], came], axis=0)
    partial = [
        dot(chip_grads[:, at], chip_rows, FIRST_FIRST) for at in range(seq_count // 2)
    ]
    token_grads = partial[0]
    for at in range(1, seq_count // 2):
        token_grads = token_grads + swap(partial[at].astype(BF), "seq", 2 * at).astype(F32)
    grad_hidden = token_grads.astype(BF)

    head_sums = sum_over_batch(jnp.dot(grads_t, hidden_all, preferred_element_type=F32))
    out_sums = sum_over_batch(jnp.dot(attended_t, grad_all, preferred_element_type=F32))
    row_block = width // batch_count
    head_part = head_sums.reshape(3, head_width, row_block).transpose(0, 2, 1)
    out_part = rows_to_owner(out_sums)[None]
    grad_weights = jnp.concatenate([head_part, out_part], axis=0)
    norm_factor = 1.0 / math.sqrt(row_count * seq_count * batch_count)
    return (grad_hidden[None], grad_weights * norm_factor)


def solution(mesh):
    placed = (
        P("batch", "seq", None),
        P("batch", "seq", None),
        P("batch", "seq", None, None),
        P(),
        P(),
        P(),
        P(),
    )
    return jax.shard_map(
        per_device,
        mesh=mesh,
        in_specs=placed,
        out_specs=(P("batch", "seq", None), P(None, "batch", "seq")),
        check_vma=False,
    )
```

```python
import functools
import math

import jax
import jax.numpy as jnp
from jax import lax
from jax.experimental import pallas as pl
from jax.experimental.pallas import tpu as pltpu
from jax.sharding import PartitionSpec as P

BLK = 128
BF = jnp.bfloat16
F32 = jnp.float32
LAST_LAST = (((1,), (1,)), ((), ()))
FIRST_FIRST = (((0,), (0,)), ((), ()))
VMEM_BYTES = 62 * 1024 * 1024
HEAVY = pl.CostEstimate(flops=1, bytes_accessed=70_000_000, transcendentals=0)
LIGHT = pl.CostEstimate(flops=1, bytes_accessed=1, transcendentals=0)


def dot(left_side, right_side, dims):
    return lax.dot_general(left_side, right_side, dims, preferred_element_type=F32)


def swap(value, axis, distance):
    count = lax.axis_size(axis)
    return lax.ppermute(value, axis, [(at, at ^ distance) for at in range(count)])


def spread(shard, axis, count):
    pieces = {0: shard}
    bit = count // 2
    while bit:
        for place in sorted(pieces):
            pieces[place | bit] = swap(pieces[place], axis, bit)
        bit //= 2
    return [pieces[place] for place in sorted(pieces)]


def side_by_side(parts):
    return parts[0] if len(parts) == 1 else jnp.concatenate(parts, axis=1)


def weight_rows_kernel(_, query_cols, key_cols, value_cols, rows):
    for at, cols in enumerate((query_cols, key_cols, value_cols)):
        rows[at * BLK : (at + 1) * BLK, :] = cols[...].T


def weight_rows(seq_index, head_width, weights):
    width = weights[0].shape[0]
    pairs = head_width // BLK
    first = jnp.reshape(seq_index * pairs, (1,)).astype(jnp.int32)
    return pl.pallas_call(
        weight_rows_kernel,
        grid_spec=pltpu.PrefetchScalarGridSpec(
            num_scalar_prefetch=1,
            grid=(pairs,),
            in_specs=[pl.BlockSpec((width, BLK), lambda pair, first: (0, first[0] + pair))] * 3,
            out_specs=pl.BlockSpec((3 * BLK, width), lambda pair, _: (pair, 0)),
        ),
        out_shape=jax.ShapeDtypeStruct((3 * head_width, width), BF),
        compiler_params=pltpu.CompilerParams(vmem_limit_bytes=VMEM_BYTES),
        cost_estimate=LIGHT,
        name="weight_rows",
    )(first, *weights)


def project_kernel(*refs, count, pairs, scale):
    tokens, grads = refs[:count], refs[count : 2 * count]
    rows, out_rows = refs[2 * count : 2 * count + 2]
    queries_t, out_grads_t, keys_t, values_t, keys, values = refs[2 * count + 2 :]
    step = tokens[0].shape[0]
    for at in range(count):
        span = slice(at * step, (at + 1) * step)
        heads_t = dot(rows[...], tokens[at][...], LAST_LAST)
        out_grads_t[:, span] = dot(out_rows[...], grads[at][...], LAST_LAST).astype(BF)
        for pair in range(pairs):
            own = slice(pair * BLK, (pair + 1) * BLK)
            base = pair * 3 * BLK
            queries_t[own, span] = heads_t[base : base + BLK].astype(BF) * scale
            key_part = heads_t[base + BLK : base + 2 * BLK]
            value_part = heads_t[base + 2 * BLK : base + 3 * BLK]
            keys_t[own, span] = key_part.astype(BF)
            values_t[own, span] = value_part.astype(BF)
            keys[span, own] = key_part.T.astype(BF)
            values[span, own] = value_part.T.astype(BF)


def project(tokens, grads, rows, out_rows, scale):
    count, step = len(tokens), tokens[0].shape[0]
    width = out_rows.shape[0]
    across = jax.ShapeDtypeStruct((width, count * step), BF)
    down = jax.ShapeDtypeStruct((count * step, width), BF)
    return pl.pallas_call(
        functools.partial(project_kernel, count=count, pairs=width // BLK, scale=scale),
        out_shape=[across] * 4 + [down] * 2,
        compiler_params=pltpu.CompilerParams(vmem_limit_bytes=VMEM_BYTES),
        cost_estimate=LIGHT,
        name="project",
    )(*tokens, *grads, rows, out_rows)


def attend(
    place_of, offsets, head_base, places, queries_t, out_grads_t, key_refs, sums, put, slots, blocks, head_size
):
    keys_t, values_t, keys, values = key_refs
    key_acc, value_acc = sums
    key_at = lax.broadcasted_iota(jnp.int32, (BLK, BLK), 0)
    query_at = lax.broadcasted_iota(jnp.int32, (BLK, BLK), 1)
    causal = key_at <= query_at
    first_head = lax.broadcasted_iota(jnp.int32, (2 * head_size, BLK), 0) < head_size
    plus = functools.partial(functools.reduce, jnp.add)
    cut = [slice(slot * BLK, (slot + 1) * BLK) for slot in range(slots)]

    for step in range(queries_t.shape[1] // BLK):
        place = places + step
        block = place_of[place]
        cols = slice(step * BLK, (step + 1) * BLK)
        pair_queries = queries_t[:, cols]
        pair_grads = out_grads_t[:, cols]
        scored = []
        for half in range(2):
            head = head_base + half
            rows = slice(half * head_size, (half + 1) * head_size)
            keep = first_head if half == 0 else ~first_head
            head_queries = jnp.where(keep, pair_queries, jnp.zeros_like(pair_queries))
            head_grads = jnp.where(keep, pair_grads, jnp.zeros_like(pair_grads))
            named, usable = [], []
            for slot in range(slots):
                offset = offsets[(head * blocks + block) * slots + slot]
                usable.append(offset <= block)
                named.append(place_of[jnp.where(offset <= block, block - offset, 0)])
            spans = [pl.ds(pl.multiple_of(at * BLK, BLK), BLK) for at in named]
            seen_keys = jnp.concatenate([keys[span, :] for span in spans], axis=0)
            seen_values = jnp.concatenate([values[span, :] for span in spans], axis=0)
            scores = jnp.dot(seen_keys, head_queries, preferred_element_type=F32)
            prob_grad = jnp.dot(seen_values, head_grads, preferred_element_type=F32)
            scores = [
                jnp.where(causal if slot == 0 else usable[slot], scores[cut[slot]], -jnp.inf)
                for slot in range(slots)
            ]
            scored.append((rows, named, spans, scores, [prob_grad[part] for part in cut]))
        parts = []
        for rows, named, spans, scores, prob_grad in scored:
            top = jnp.max(functools.reduce(jnp.maximum, scores), axis=0, keepdims=True)
            raised = [jnp.exp(part - top) for part in scores]
            total = jnp.sum(plus(raised), axis=0, keepdims=True)
            inverse = 1.0 / total
            probs = [part * inverse for part in raised]
            probs_half = jnp.concatenate([part.astype(BF) for part in probs], axis=0)
            delta = jnp.sum(
                plus([part * grad for part, grad in zip(probs, prob_grad)]), axis=0, keepdims=True
            )
            score_grad = jnp.concatenate(
                [(part * (grad - delta)).astype(BF) for part, grad in zip(probs, prob_grad)], axis=0
            )
            seen_values_t = side_by_side([values_t[rows, span] for span in spans])
            seen_keys_t = side_by_side([keys_t[rows, span] for span in spans])
            attended = jnp.dot(seen_values_t, probs_half, preferred_element_type=F32)
            query_grad = jnp.dot(seen_keys_t, score_grad, preferred_element_type=F32)
            put(rows, cols, attended, query_grad * (1.0 / math.sqrt(head_size)))
            value_part = dot(out_grads_t[rows, cols], probs_half, LAST_LAST)
            key_part = dot(queries_t[rows, cols], score_grad, LAST_LAST)
            parts.append((rows, named, key_part, value_part))
        for rows, named, key_part, value_part in parts:
            for at, part in zip(named, cut):
                key_acc[at, rows, :] += key_part[:, part]
                value_acc[at, rows, :] += value_part[:, part]


def own_half_kernel(place_of, offsets, *refs, count, slots, blocks, head_size, scale):
    tokens = refs[:count]
    (rows, queries_t, out_grads_t, keys_in, values_in, keys_down, values_down) = refs[count : count + 7]
    (
        later_queries_t,
        keys_t,
        values_t,
        keys,
        values,
        attended_t,
        query_grad_t,
        key_acc_out,
        value_acc_out,
    ) = refs[count + 7 :]
    pair = pl.program_id(0)
    key_acc, value_acc = key_acc_out.at[0], value_acc_out.at[0]
    half = queries_t.shape[1]
    step = tokens[0].shape[0]
    keys_t[:, :half] = keys_in[...]
    values_t[:, :half] = values_in[...]
    keys[:half, :] = keys_down[...]
    values[:half, :] = values_down[...]
    for at in range(count):
        span = slice(at * step, (at + 1) * step)
        whole = slice(half + at * step, half + (at + 1) * step)
        heads_t = dot(rows[...], tokens[at][...], LAST_LAST)
        later_queries_t[:, span] = heads_t[:BLK].astype(BF) * scale
        keys_t[:, whole] = heads_t[BLK : 2 * BLK].astype(BF)
        values_t[:, whole] = heads_t[2 * BLK :].astype(BF)
        keys[whole, :] = heads_t[BLK : 2 * BLK].T.astype(BF)
        values[whole, :] = heads_t[2 * BLK :].T.astype(BF)
    key_acc[...] = jnp.zeros(key_acc.shape, F32)
    value_acc[...] = jnp.zeros(value_acc.shape, F32)

    def put(at_rows, cols, attended, query_grad):
        attended_t[at_rows, cols] = attended.astype(BF)
        query_grad_t[at_rows, cols] = query_grad.astype(BF)

    attend(
        place_of,
        offsets,
        2 * pair,
        0,
        queries_t,
        out_grads_t,
        (keys_t, values_t, keys, values),
        (key_acc, value_acc),
        put,
        slots,
        blocks,
        head_size,
    )


def own_half(place_of, offsets, tokens, rows, projected):
    queries_t = projected[0]
    width, half = queries_t.shape
    heads, blocks, slots = offsets.shape
    head_size = width // heads
    pairs = width // BLK
    total = blocks * BLK
    model = rows.shape[1]
    whole_piece = pl.BlockSpec(tokens[0].shape, lambda pair, *_: (0, 0))
    half_across = pl.BlockSpec((BLK, half), lambda pair, *_: (pair, 0))
    across = pl.BlockSpec((BLK, total), lambda pair, *_: (pair, 0))
    half_down = pl.BlockSpec((half, BLK), lambda pair, *_: (0, pair))
    down = pl.BlockSpec((total, BLK), lambda pair, *_: (0, pair))
    sums = pl.BlockSpec((1, blocks, BLK, BLK), lambda pair, *_: (pair, 0, 0, 0))
    shape = jax.ShapeDtypeStruct
    return pl.pallas_call(
        functools.partial(
            own_half_kernel,
            count=len(tokens),
            slots=slots,
            blocks=blocks,
            head_size=head_size,
            scale=1.0 / math.sqrt(head_size),
        ),
        grid_spec=pltpu.PrefetchScalarGridSpec(
            num_scalar_prefetch=2,
            grid=(pairs,),
            in_specs=[whole_piece] * len(tokens)
            + [pl.BlockSpec((3 * BLK, model), lambda pair, *_: (pair, 0))]
            + [half_across] * 4
            + [half_down] * 2,
            out_specs=[half_across, across, across, down, down, half_across, half_across, sums, sums],
        ),
        out_shape=[
            shape((width, half), BF),
            shape((width, total), BF),
            shape((width, total), BF),
            shape((total, width), BF),
            shape((total, width), BF),
            shape((width, half), BF),
            shape((width, half), BF),
            shape((pairs, blocks, BLK, BLK), F32),
            shape((pairs, blocks, BLK, BLK), F32),
        ],
        compiler_params=pltpu.CompilerParams(vmem_limit_bytes=VMEM_BYTES),
        cost_estimate=LIGHT,
        name="own_half",
    )(place_of, offsets.reshape(-1), *tokens, rows, *projected)


def later_half_kernel(place_of, offsets, col_order, *refs, count, pair, slots, blocks, head_size):
    tokens_at, grads_at = refs[:count], refs[count : 2 * count]
    (
        out_rows,
        queries_t,
        keys_t,
        values_t,
        keys,
        values,
        attended_first,
        query_grad_first,
        key_first,
        value_first,
        stay,
        leave,
        *terms,
        attended_t,
        out_grads_t,
        key_acc,
        value_acc,
        tokens_here,
        grads_here,
        arrived,
    ) = refs[2 * count :]
    half = queries_t.shape[1]
    near = count // 2
    tokens = [tokens_here.at[at] for at in range(count)]
    grads = [grads_here.at[at] for at in range(count)]
    step = grads[0].shape[0]

    def fetch(sources, targets, first_sem):
        copies = [
            pltpu.make_async_copy(source, target, arrived.at[first_sem + at])
            for at, (source, target) in enumerate(zip(sources, targets))
        ]
        for copy in copies:
            copy.start()
        return copies

    first_copies = fetch(grads_at[near:], grads[near:], 0)
    later_copies = fetch((*tokens_at, *grads_at[:near]), (*tokens, *grads[:near]), near)
    for copy in first_copies:
        copy.wait()
    for at in range(near):
        span = slice(at * step, (at + 1) * step)
        out_grads_t[:, span] = dot(out_rows[...], grads[near + at][...], LAST_LAST).astype(BF)
    key_acc[...] = key_first[0]
    value_acc[...] = value_first[0]
    attended_t[:, :half] = attended_first[...]

    def columns(place, at):
        left = place // 2 * step + at
        return (leave if place % 2 else stay), slice(left, left + BLK)

    for at in range(0, half, BLK):
        target, cols = columns(at // step, at % step)
        target[:BLK, cols] = query_grad_first[:, at : at + BLK]

    def put(at_rows, cols, attended, query_grad):
        attended_t[at_rows, half + cols.start : half + cols.stop] = attended.astype(BF)
        target, placed = columns(near + cols.start // step, cols.start % step)
        target[at_rows, placed] = query_grad.astype(BF)

    attend(
        place_of,
        offsets,
        2 * pair,
        blocks // 2,
        queries_t,
        out_grads_t,
        (keys_t, values_t, keys, values),
        (key_acc, value_acc),
        put,
        slots,
        blocks,
        head_size,
    )
    for at in range(blocks):
        target, cols = columns(at * BLK // step, at * BLK % step)
        target[BLK : 2 * BLK, cols] = key_acc[at].astype(BF)
        target[2 * BLK :, cols] = value_acc[at].astype(BF)

    for copy in later_copies:
        copy.wait()
    stay_rows, leave_rows, attended_rows = stay[...], leave[...], attended_t[...]
    width = tokens[0].shape[1]
    for col in range(0, width, 2 * BLK):
        spans = [
            pl.ds(pl.multiple_of(col_order[col // BLK + side] * BLK, BLK), BLK) for side in range(2)
        ]

        def taken(pieces):
            return jnp.concatenate(
                [side_by_side([piece[:, span] for span in spans]) for piece in pieces], axis=0
            )

        head_terms = jnp.dot(stay_rows, taken(tokens[0::2]), preferred_element_type=F32)
        head_terms += jnp.dot(leave_rows, taken(tokens[1::2]), preferred_element_type=F32)
        out_terms = jnp.dot(attended_rows, taken(grads), preferred_element_type=F32)
        first_rows, last_rows = terms[:2] if col < width // 2 else terms[2:]
        cols = slice(col % (width // 2), col % (width // 2) + 2 * BLK)
        first_rows[:BLK, cols] = out_terms.astype(first_rows.dtype)
        first_rows[BLK:, cols] = head_terms[:BLK].astype(first_rows.dtype)
        last_rows[:, cols] = head_terms[BLK:].astype(last_rows.dtype)


def later_half(place_of, offsets, col_order, tokens, grads, out_rows, pair, first):
    (queries_t, keys_t, values_t, keys, values, attended_t, query_grad_t, key_acc, value_acc) = first
    width, half = queries_t.shape
    heads, blocks, slots = offsets.shape
    head_size = width // heads
    total = blocks * BLK
    model = out_rows.shape[1]
    whole_piece = pl.BlockSpec(memory_space=pl.ANY)
    half_across = pl.BlockSpec((BLK, half), lambda *_: (pair, 0))
    across = pl.BlockSpec((BLK, total), lambda *_: (pair, 0))
    down = pl.BlockSpec((total, BLK), lambda *_: (0, pair))
    sums = pl.BlockSpec((1, blocks, BLK, BLK), lambda *_: (pair, 0, 0, 0))
    shape = jax.ShapeDtypeStruct
    results = [
        shape((3 * BLK, half), BF),
        shape((3 * BLK, half), BF),
        shape((2 * BLK, model // 2), BF),
        shape((2 * BLK, model // 2), BF),
        shape((2 * BLK, model // 2), F32),
        shape((2 * BLK, model // 2), F32),
    ]
    return pl.pallas_call(
        functools.partial(
            later_half_kernel,
            count=len(grads),
            pair=pair,
            slots=slots,
            blocks=blocks,
            head_size=head_size,
        ),
        grid_spec=pltpu.PrefetchScalarGridSpec(
            num_scalar_prefetch=3,
            grid=(1,),
            in_specs=[whole_piece] * (2 * len(grads))
            + [pl.BlockSpec((BLK, model), lambda *_: (pair, 0))]
            + [half_across, across, across, down, down, half_across, half_across, sums, sums],
            out_specs=[pl.BlockSpec(result.shape, lambda *_: (0, 0)) for result in results],
            scratch_shapes=[pltpu.VMEM((BLK, total), BF), pltpu.VMEM((BLK, half), BF)]
            + [pltpu.VMEM((blocks, BLK, BLK), F32)] * 2
            + [pltpu.VMEM((len(grads), *grads[0].shape), BF)] * 2
            + [pltpu.SemaphoreType.DMA((2 * len(grads),))],
        ),
        out_shape=results,
        compiler_params=pltpu.CompilerParams(vmem_limit_bytes=VMEM_BYTES),
        cost_estimate=LIGHT,
        name="later_half",
    )(place_of, offsets.reshape(-1), col_order, *tokens, *grads, out_rows, *first)


def finish_kernel(*refs):
    total = refs[0][...]
    for part in refs[1:-1]:
        total = total + part[...].astype(F32)
    refs[-1][...] = total.astype(BF)


def finish(own, came):
    return pl.pallas_call(
        finish_kernel,
        out_shape=jax.ShapeDtypeStruct(own.shape, BF),
        compiler_params=pltpu.CompilerParams(vmem_limit_bytes=VMEM_BYTES),
        cost_estimate=HEAVY,
        name="finish",
    )(own, *came)


def halves(pieces, low):
    kept = {place: part for place, part in pieces.items() if (place // low) % 2 == 0}
    return side_by_side([pieces[place + low].astype(BF) for place in kept]), kept


def joined(kept, came):
    block = came.shape[1] // len(kept)
    return {
        place: part + came[:, at * block : (at + 1) * block].astype(F32)
        for at, (place, part) in enumerate(kept.items())
    }


def tied(values, others):
    return list(lax.optimization_barrier((*values, *others))[: len(values)])


def rows_to_owner(block_sum):
    seq_count, batch_count = lax.axis_size("seq"), lax.axis_size("batch")
    batch_at = lax.axis_index("batch")
    ratio = batch_count // seq_count
    height, width = block_sum.shape[0] // ratio, block_sum.shape[1]
    placed = jnp.zeros((height, ratio * width), F32)
    for turn in range(ratio):
        moves = []
        for b in range(batch_count):
            for s in range(seq_count):
                target = (b // ratio) * batch_count + ratio * s + (b + turn) % ratio
                moves.append((s * batch_count + b, target))
        piece = lax.dynamic_slice(
            block_sum, (((batch_at + turn) % ratio) * height, 0), (height, width)
        )
        came = lax.ppermute(piece, ("seq", "batch"), moves)
        placed = lax.dynamic_update_slice(
            placed, came, (0, ((batch_at - turn) % ratio) * width)
        )
    return placed


def per_device(hidden, grad_out, block_offsets, w_query, w_key, w_value, w_out):
    tokens = hidden[0]
    grad_rows = grad_out[0]
    offsets = block_offsets[0]
    row_count, width = tokens.shape
    seq_count = lax.axis_size("seq")
    batch_count = lax.axis_size("batch")
    seq_at = lax.axis_index("seq")
    head_width = width // seq_count
    head_size = head_width // offsets.shape[0]
    pairs = head_width // BLK
    half_count = seq_count // 2

    weights = (w_query, w_key, w_value)
    rows = weight_rows(seq_at, head_width, weights)
    out_rows = lax.dynamic_slice(w_out, (seq_at * head_width, 0), (head_width, width))

    shard_blocks = row_count // BLK
    block_at = jnp.arange(shard_blocks * seq_count, dtype=jnp.int32)
    place_of = ((block_at // shard_blocks) ^ seq_at) * shard_blocks + block_at % shard_blocks

    near_tokens = spread(tokens, "seq", half_count)
    near_grads = spread(grad_rows, "seq", half_count)
    projected = project(near_tokens, near_grads, rows, out_rows, 1.0 / math.sqrt(head_size))
    far_tokens = swap(tokens, "seq", half_count)
    mate_rows = weight_rows(seq_at ^ 1, head_width, weights)
    far_grads, far_tokens, mate_rows, *projected = lax.optimization_barrier(
        (grad_rows, far_tokens, mate_rows, *projected)
    )
    far_grads = swap(far_grads, "seq", half_count)
    far_tokens = spread(far_tokens, "seq", half_count)
    first = own_half(place_of, offsets, far_tokens, rows, projected)
    far_grads, *first = lax.optimization_barrier((far_grads, *first))
    far_grads = spread(far_grads, "seq", half_count)
    all_tokens, all_grads = near_tokens + far_tokens, near_grads + far_grads

    col_block = width // batch_count
    direct = col_block == BLK
    relative = [*range(1, batch_count, 2), *range(0, batch_count, 2)]
    col_order = jnp.arange(width // BLK, dtype=jnp.int32)
    if direct:
        col_order = jnp.stack([lax.axis_index("batch") ^ place for place in relative]).astype(jnp.int32)
    batch_at = lax.axis_index("batch")

    even = range(0, batch_count, 2)

    def begin(sent_terms, kept_terms):
        if direct:
            return sent_terms, {p: kept_terms[:, p // 2 * BLK : (p // 2 + 1) * BLK] for p in even}
        terms = jnp.concatenate([sent_terms.astype(F32), kept_terms], axis=1)
        pieces = [
            lax.dynamic_slice(
                terms, (0, (batch_at ^ p) * col_block), (terms.shape[0], col_block)
            )
            for p in range(batch_count)
        ]
        return side_by_side([pieces[p + 1].astype(BF) for p in even]), {p: pieces[p] for p in even}

    stayed, left, groups = [], [], []
    for pair in range(pairs):
        stay, leave, *terms = later_half(
            place_of, offsets, col_order, all_tokens, all_grads, out_rows, pair, first
        )
        stayed.append(stay)
        left.append(leave)
        if pair < pairs - 1:
            terms = [jnp.concatenate(terms[:2], axis=0), jnp.concatenate(terms[2:], axis=0)]
        count = len(terms) // 2
        for at in range(count):
            goes, kept = begin(terms[at], terms[count + at])
            if at:
                goes, *came = tied([goes, *came], [])
            groups.append((swap(goes, "batch", 1), kept))
            if pair == pairs - 1 and not at:
                came = [swap(leave, "seq", 1) for leave in left]

    stayed, came = jnp.concatenate(stayed, axis=0), jnp.concatenate(came, axis=0)
    partial = []
    for at in range(half_count):
        cols = slice(at * row_count, (at + 1) * row_count)
        partial.append(
            dot(stayed[:, cols], rows, FIRST_FIRST) + dot(came[:, cols], mate_rows, FIRST_FIRST)
        )
    sent = [partial[at].astype(BF) for at in range(1, half_count)]
    token_parts = [swap(part, "seq", 2 * at) for at, part in enumerate(sent, 1)]
    came_terms = [part for part, _ in groups]
    came_terms[pairs - 1] = tied([came_terms[pairs - 1]], sent)[0]

    pieces = [joined(kept, came) for (_, kept), came in zip(groups, came_terms)]
    low = 2
    while low < batch_count:
        for at, parts in enumerate(pieces):
            goes, kept = halves(parts, low)
            if at == pairs - 1 and low * 2 == batch_count:
                goes = tied([goes], [came_terms[pairs]])[0]
            pieces[at] = joined(kept, swap(goes, "batch", low))
        low *= 2
    sums = [parts[0] for parts in pieces]
    out_sums = jnp.concatenate([part[:BLK] for part in sums[:pairs]], axis=0)
    out_sums = tied([out_sums], token_parts)[0]
    out_part = rows_to_owner(out_sums)[None]
    grad_hidden = finish(partial[0], token_parts)
    sums = [*sums[: pairs - 1], jnp.concatenate(sums[pairs - 1 :], axis=0)]
    sums[0], out_part = tied([sums[0], out_part], [grad_hidden])
    row_block = width // batch_count
    head_part = jnp.stack([part[BLK:].reshape(3, BLK, row_block) for part in sums], axis=1)
    head_part = head_part.reshape(3, head_width, row_block).transpose(0, 2, 1)
    grad_weights = jnp.concatenate([head_part, out_part], axis=0)
    norm_factor = 1.0 / math.sqrt(row_count * seq_count * batch_count)
    return (grad_hidden[None], grad_weights * norm_factor)


def solution(mesh):
    placed = (
        P("batch", "seq", None),
        P("batch", "seq", None),
        P("batch", "seq", None, None),
        P(),
        P(),
        P(),
        P(),
    )
    return jax.shard_map(
        per_device,
        mesh=mesh,
        in_specs=placed,
        out_specs=(P("batch", "seq", None), P(None, "batch", "seq")),
        check_vma=False,
    )
```

```python
import functools
import math

import jax
import jax.numpy as jnp
from jax import lax
from jax.experimental import pallas as pl
from jax.experimental.pallas import tpu as pltpu
from jax.sharding import PartitionSpec as P

BLK = 128
BF = jnp.bfloat16
F32 = jnp.float32
LAST_LAST = (((1,), (1,)), ((), ()))
VMEM_BYTES = 66584576
LIGHT = pl.CostEstimate(flops=1, bytes_accessed=1, transcendentals=0)


def dot(left_side, right_side, dims):
    return lax.dot_general(left_side, right_side, dims, preferred_element_type=F32)


def swap(value, axis, distance):
    count = lax.axis_size(axis)
    return lax.ppermute(value, axis, [(at, at ^ distance) for at in range(count)])


def spread(shard, axis, count):
    pieces = {0: shard}
    bit = count // 2
    while bit:
        for place in sorted(pieces):
            pieces[place | bit] = swap(pieces[place], axis, bit)
        bit //= 2
    return [pieces[place] for place in sorted(pieces)]


def side_by_side(parts):
    return parts[0] if len(parts) == 1 else jnp.concatenate(parts, axis=1)


class Held:
    def __init__(self, source, target, arrived):
        self.target, self.copy, self.there = target, None, False
        self.copy = pltpu.make_async_copy(source, target, arrived)
        self.copy.start()

    def __call__(self):
        if not self.there:
            self.copy.wait()
            self.there = True
        return self.target


class Sent:
    def __init__(self, outs, held, left):
        self.outs, self.held, self.left, self.copies = outs, held, left, []

    def __getitem__(self, at):
        return self.held[at]

    def start(self, at, part=None):
        source, target = self.held[at], self.outs[at]
        if part is not None:
            source, target = source.at[part], target.at[part]
        copy = pltpu.make_async_copy(source, target, self.left.at[len(self.copies)])
        copy.start()
        self.copies.append(copy)

    def finish(self):
        for copy in self.copies:
            copy.wait()


def part_shape(shape, part):
    if part is None:
        return shape
    kept = []
    for size, index in zip(shape, part):
        if isinstance(index, slice):
            kept.append(len(range(*index.indices(size))))
        elif not isinstance(index, int):
            kept.append(index.size)
    return tuple(kept)


def run(body, name, scalars, operands, results, scratch, most_copies):
    arrays = [array for array, _ in operands]
    taken = [
        part_shape(array.shape, part([None] * 99, 0) if callable(part) else part)
        for array, part in operands
    ]
    n, k, m = len(scalars), len(arrays), len(results)

    def kernel(*refs):
        given, sources, outs = refs[:n], refs[n : n + k], refs[n + k : n + k + m]
        refs = refs[n + k + m :]
        targets, held, own, (arrived, left) = refs[:k], refs[k : k + m], refs[k + m : -2], refs[-2:]
        ready = []
        for at, (source, (_, part)) in enumerate(zip(sources, operands)):
            if callable(part):
                part = part(given, None)
            source = source if part is None else source.at[part]
            ready.append(Held(source, targets[at], arrived.at[at]))
        sent = Sent(outs, held, left)
        body(given, ready, sent, *own)
        sent.finish()

    return pl.pallas_call(
        kernel,
        in_specs=[pl.BlockSpec(memory_space=pltpu.SMEM)] * n + [pl.BlockSpec(memory_space=pl.ANY)] * k,
        out_specs=[pl.BlockSpec(memory_space=pl.ANY)] * m,
        out_shape=[jax.ShapeDtypeStruct(*result) for result in results],
        scratch_shapes=[pltpu.VMEM(shape, array.dtype) for shape, array in zip(taken, arrays)]
        + [pltpu.VMEM(*result) for result in results]
        + scratch
        + [pltpu.SemaphoreType.DMA((k,)), pltpu.SemaphoreType.DMA((most_copies,))],
        compiler_params=pltpu.CompilerParams(vmem_limit_bytes=VMEM_BYTES),
        cost_estimate=LIGHT,
        name=name,
    )(*scalars, *arrays)


def whole(arrays):
    return [(array, None) for array in arrays]


def weight_rows(seq_index, head_width, weights):
    width, count = weights[0].shape[0], len(weights)
    pairs = head_width // BLK
    first = jnp.reshape(seq_index * head_width, (1,)).astype(jnp.int32)

    def cols(scalars, dry):
        start = 0 if dry is not None else pl.multiple_of(scalars[0][0], BLK)
        return (slice(0, width), pl.ds(start, head_width))

    def body(_, ready, sent):
        rows = sent[0]
        for at in range(count):
            taken = ready[at]()
            for pair in range(pairs):
                base = (pair * count + at) * BLK
                rows[base : base + BLK, :] = taken[:, pair * BLK : (pair + 1) * BLK].T
        sent.start(0)

    operands = [(weight, cols) for weight in weights]
    return run(body, "weight_rows", [first], operands, [((count * head_width, width), BF)], [], 1)[0]


def out_rows_part(blocks, more, height, model):
    def part(scalars, dry):
        start = 0 if dry is not None else pl.multiple_of(scalars[0][blocks] + more, BLK)
        return (pl.ds(start, height), slice(0, model))

    return part


def project(plan, blocks, tokens, grads, rows, out_weight, scale):
    count, (step, model) = len(tokens), tokens[0].shape
    width = rows.shape[0] // 3
    pairs = width // BLK
    across, down = ((width, count * step), BF), ((count * step, width), BF)

    def body(_, ready, sent):
        rows, out_rows, far_rows = ready[0], ready[1], ready[2 : 2 + count]
        tokens_here, grads_here = ready[2 + count : 2 + 2 * count], ready[2 + 2 * count :]
        queries_t, out_grads_t, keys_t, values_t, keys, values = (sent[at] for at in range(6))
        own_grads = grads_here[0]()[...]
        for at in range(count):
            sent[6 + at][...] = dot(far_rows[at]()[...], own_grads, LAST_LAST).astype(BF)
            sent.start(6 + at)
        for at in range(2):
            sent[6 + count + at][...] = own_grads[at * step // 2 : (at + 1) * step // 2]
            sent.start(6 + count + at)
        for at in range(count):
            span = slice(at * step, (at + 1) * step)
            heads_t = dot(rows()[...], tokens_here[at]()[...], LAST_LAST)
            for pair in range(pairs):
                own = slice(pair * BLK, (pair + 1) * BLK)
                base = pair * 3 * BLK
                queries_t[own, span] = heads_t[base : base + BLK].astype(BF) * scale
                key_part = heads_t[base + BLK : base + 2 * BLK]
                value_part = heads_t[base + 2 * BLK : base + 3 * BLK]
                keys_t[own, span] = key_part.astype(BF)
                values_t[own, span] = value_part.astype(BF)
                keys[span, own] = key_part.T.astype(BF)
                values[span, own] = value_part.T.astype(BF)
        for at in (0, 2, 3, 4, 5):
            sent.start(at)
        for at in range(count):
            span = slice(at * step, (at + 1) * step)
            out_grads_t[:, span] = dot(out_rows()[...], grads_here[at]()[...], LAST_LAST).astype(BF)
        sent.start(1)

    operands = [(rows, None), (out_weight, out_rows_part(blocks, 0, width, model))]
    operands += [
        (out_weight, out_rows_part(blocks + 1 + at, 0, width, model)) for at in range(count)
    ]
    operands += whole(tokens) + whole(grads)
    results = [across] * 4 + [down] * 2 + [((width, step), BF)] * count
    results += [((step // 2, model), BF)] * 2
    return run(body, "project", [plan], operands, results, [], 8 + count)


def attend(
    place_of, offsets, head_base, places, queries_t, out_grads_t, key_refs, sums, put, slots, blocks, head_size
):
    keys_t, values_t, keys, values = key_refs
    key_acc, value_acc = sums
    key_at = lax.broadcasted_iota(jnp.int32, (BLK, BLK), 0)
    query_at = lax.broadcasted_iota(jnp.int32, (BLK, BLK), 1)
    causal = key_at <= query_at
    first_head = lax.broadcasted_iota(jnp.int32, (2 * head_size, BLK), 0) < head_size
    plus = functools.partial(functools.reduce, jnp.add)
    cut = [slice(slot * BLK, (slot + 1) * BLK) for slot in range(slots)]

    for step in range(queries_t.shape[1] // BLK):
        place = places + step
        block = place_of[place]
        cols = slice(step * BLK, (step + 1) * BLK)
        pair_queries = queries_t[:, cols]
        pair_grads = out_grads_t[:, cols]
        scored = []
        for half in range(2):
            head = head_base + half
            rows = slice(half * head_size, (half + 1) * head_size)
            keep = first_head if half == 0 else ~first_head
            head_queries = jnp.where(keep, pair_queries, jnp.zeros_like(pair_queries))
            head_grads = jnp.where(keep, pair_grads, jnp.zeros_like(pair_grads))
            named, usable = [], []
            for slot in range(slots):
                offset = offsets[(head * blocks + block) * slots + slot]
                usable.append(offset <= block)
                named.append(place_of[jnp.where(offset <= block, block - offset, 0)])
            spans = [pl.ds(pl.multiple_of(at * BLK, BLK), BLK) for at in named]
            seen_keys = jnp.concatenate([keys[span, :] for span in spans], axis=0)
            seen_values = jnp.concatenate([values[span, :] for span in spans], axis=0)
            scores = jnp.dot(seen_keys, head_queries, preferred_element_type=F32)
            prob_grad = jnp.dot(seen_values, head_grads, preferred_element_type=F32)
            scores = [
                jnp.where(causal if slot == 0 else usable[slot], scores[cut[slot]], -jnp.inf)
                for slot in range(slots)
            ]
            scored.append((rows, named, spans, scores, [prob_grad[part] for part in cut]))
        parts = []
        for rows, named, spans, scores, prob_grad in scored:
            top = jnp.max(functools.reduce(jnp.maximum, scores), axis=0, keepdims=True)
            raised = [jnp.exp(part - top) for part in scores]
            total = jnp.sum(plus(raised), axis=0, keepdims=True)
            inverse = 1.0 / total
            probs = [part * inverse for part in raised]
            probs_half = jnp.concatenate([part.astype(BF) for part in probs], axis=0)
            delta = jnp.sum(
                plus([part * grad for part, grad in zip(probs, prob_grad)]), axis=0, keepdims=True
            )
            score_grad = jnp.concatenate(
                [(part * (grad - delta)).astype(BF) for part, grad in zip(probs, prob_grad)], axis=0
            )
            seen_values_t = side_by_side([values_t[rows, span] for span in spans])
            seen_keys_t = side_by_side([keys_t[rows, span] for span in spans])
            attended = jnp.dot(seen_values_t, probs_half, preferred_element_type=F32)
            query_grad = jnp.dot(seen_keys_t, score_grad, preferred_element_type=F32)
            put(rows, cols, attended, query_grad * (1.0 / math.sqrt(head_size)))
            value_part = dot(out_grads_t[rows, cols], probs_half, LAST_LAST)
            key_part = dot(queries_t[rows, cols], score_grad, LAST_LAST)
            parts.append((rows, named, key_part, value_part))
        for rows, named, key_part, value_part in parts:
            for at, part in zip(named, cut):
                key_acc[at, rows, :] += key_part[:, part]
                value_acc[at, rows, :] += value_part[:, part]


def own_half(plan, offsets, tokens, rows, projected):
    width, half = projected[0].shape
    heads, blocks, slots = offsets.shape
    head_size, pairs, total, count = width // heads, width // BLK, blocks * BLK, len(tokens)
    half_across, across, down = ((width, half), BF), ((width, total), BF), ((total, width), BF)
    sums = ((pairs, blocks, BLK, BLK), F32)
    scale = 1.0 / math.sqrt(head_size)

    def body(scalars, ready, sent):
        rows, tokens_here = ready[0], ready[1 : 1 + count]
        queries_t, out_grads_t, keys_in, values_in, keys_down, values_down = ready[1 + count :]
        later_queries_t, keys_t, values_t, keys, values = (sent[at] for at in range(5))
        attended_t, query_grad_t, key_acc, value_acc = (sent[at] for at in range(5, 9))
        key_acc[...] = jnp.zeros(key_acc.shape, F32)
        value_acc[...] = jnp.zeros(value_acc.shape, F32)
        step = tokens[0].shape[0]
        for at in range(count):
            span = slice(at * step, (at + 1) * step)
            placed = slice(half + at * step, half + (at + 1) * step)
            for pair in range(pairs):
                own = slice(pair * BLK, (pair + 1) * BLK)
                pair_rows = rows()[pair * 3 * BLK : (pair + 1) * 3 * BLK, :]
                heads_t = dot(pair_rows, tokens_here[at]()[...], LAST_LAST)
                later_queries_t[own, span] = heads_t[:BLK].astype(BF) * scale
                keys_t[own, placed] = heads_t[BLK : 2 * BLK].astype(BF)
                values_t[own, placed] = heads_t[2 * BLK :].astype(BF)
                keys[placed, own] = heads_t[BLK : 2 * BLK].T.astype(BF)
                values[placed, own] = heads_t[2 * BLK :].T.astype(BF)
        keys_t[:, :half] = keys_in()[...]
        values_t[:, :half] = values_in()[...]
        keys[:half, :] = keys_down()[...]
        values[:half, :] = values_down()[...]
        for at in range(5):
            sent.start(at)

        for pair in range(pairs):
            own = slice(pair * BLK, (pair + 1) * BLK)

            def put(at_rows, cols, attended, query_grad):
                placed = slice(own.start + at_rows.start, own.start + at_rows.stop)
                attended_t[placed, cols] = attended.astype(BF)
                query_grad_t[placed, cols] = query_grad.astype(BF)

            attend(
                scalars[0],
                scalars[1],
                2 * pair,
                0,
                queries_t().at[own, :],
                out_grads_t().at[own, :],
                (keys_t.at[own, :], values_t.at[own, :], keys.at[:, own], values.at[:, own]),
                (key_acc.at[pair], value_acc.at[pair]),
                put,
                slots,
                blocks,
                head_size,
            )
            for at in (5, 6):
                sent.start(at, (own, slice(0, half)))
            for at in (7, 8):
                sent.start(at, (pair,))

    results = [half_across, across, across, down, down, half_across, half_across, sums, sums]
    operands = whole([rows, *tokens, *projected])
    return run(
        body, "own_half", [plan, offsets.reshape(-1)], operands, results, [], 5 + 4 * pairs
    )


def later_half(
    plan, offsets, order_at, far_grads_t, pair, first, tokens, grads, attended, before, rows, mate_rows
):
    width, half = first[0].shape
    heads, blocks, slots = offsets.shape
    head_size, total = width // heads, blocks * BLK
    near, step = len(far_grads_t), far_grads_t[0].shape[1]
    model, count = tokens[0].shape[1], len(tokens)
    own = slice(pair * BLK, (pair + 1) * BLK)
    across, half_across, down = (own, slice(0, total)), (own, slice(0, half)), (slice(0, total), own)
    last, final = bool(grads), rows is not None

    def body(scalars, ready, sent, out_grads_t, stay, leave):
        plan = scalars[0]
        queries_t, keys_t, values_t, keys, values, key_acc, value_acc = (
            part() for part in ready[near : near + 7]
        )
        query_grad_first = ready[near + 7]
        tokens_here = ready[near + 8 : near + 8 + count]
        grads_here = ready[near + 8 + count : near + 8 + count + len(grads)]
        attended_here = ready[near + 8 + count + len(grads) :]
        attended_here, shares_here = attended_here[: len(attended)], attended_here[len(attended) :]
        attended_t = sent[0]
        for at in range(near):
            out_grads_t[:, at * step : (at + 1) * step] = ready[at]()[...]

        def columns(place, at):
            left = place // 2 * step + at
            return (leave if place % 2 else stay), slice(left, left + BLK)

        def put(at_rows, cols, attended, query_grad):
            attended_t[at_rows, cols] = attended.astype(BF)
            target, placed = columns(near + cols.start // step, cols.start % step)
            target[at_rows, placed] = query_grad.astype(BF)

        attend(
            plan,
            scalars[1],
            2 * pair,
            blocks // 2,
            queries_t,
            out_grads_t,
            (keys_t, values_t, keys, values),
            (key_acc, value_acc),
            put,
            slots,
            blocks,
            head_size,
        )
        if not last:
            sent.start(0)
        for at in range(0, half, BLK):
            target, cols = columns(at // step, at % step)
            target[:BLK, cols] = query_grad_first()[:, at : at + BLK]
        for at in range(blocks):
            target, cols = columns(at * BLK // step, at * BLK % step)
            target[BLK : 2 * BLK, cols] = key_acc[at].astype(BF)
            target[2 * BLK :, cols] = value_acc[at].astype(BF)
        for at, held in ((1, stay), (2, leave)):
            for cols in range(0, half, BLK):
                sent[at][cols : cols + BLK, :] = held[:, cols : cols + BLK].T
            sent.start(at)
        if final:
            parts = [(sent[1], shares_here[-1], pair)]
            parts += [
                (shares_here[2 * at + side], shares_here[-1 - side], at)
                for at in range(len(before))
                for side in (1, 0)
            ]
            lefts = [(left() if isinstance(left, Held) else left)[step:, :] for left, _, _ in parts]
            left = jnp.concatenate(lefts, axis=1)
            model_n = rows.shape[1]
            for col in range(0, model_n, 2 * BLK):
                cols = slice(col, col + 2 * BLK)
                held = [
                    right()[at * 3 * BLK : (at + 1) * 3 * BLK, cols] for _, right, at in parts
                ]
                sent[5][:, cols] = jnp.dot(
                    left, jnp.concatenate(held, axis=0), preferred_element_type=F32
                )
            sent.start(5)

        def put_terms(at, lefts, rights):
            pieces = [[part() for part in right] for right in rights]
            for col in range(0, model, 2 * BLK):
                spans = [
                    pl.ds(pl.multiple_of(plan[order_at + col // BLK + side] * BLK, BLK), BLK)
                    for side in range(2)
                ]
                terms = 0.0
                for left, right in zip(lefts, pieces):
                    cut = [side_by_side([part[:, span] for span in spans]) for part in right]
                    terms += jnp.dot(
                        left, jnp.concatenate(cut, axis=0), preferred_element_type=F32
                    )
                target, cols = sent[at + col // (model // 2)], col % (model // 2)
                target[:, cols : cols + 2 * BLK] = terms.astype(target.dtype)
                if cols + 2 * BLK == model // 2:
                    sent.start(at + col // (model // 2))

        if last:
            lefts = [attended_here[0]()[...]]
            lefts.append(
                jnp.concatenate([part()[...] for part in attended_here[1:]] + [attended_t[...]], axis=0)
            )
            pieces = [[part() for part in grads_here[:near]], [part() for part in grads_here[near:]]]
            own_rows = plan[order_at + model // BLK + model // width]
            for at in range(model // width):
                span = pl.ds(
                    pl.multiple_of(plan[order_at + model // BLK + at] * width, width), width
                )
                terms = 0.0
                for left, right in zip(lefts, pieces):
                    taken = jnp.concatenate([part[:, span] for part in right], axis=0)
                    terms += jnp.dot(left, taken, preferred_element_type=F32)
                cols = slice(at * width, (at + 1) * width)
                sent[6][:, cols] = jnp.where(own_rows == 0, terms[BLK:], terms[:BLK]).astype(BF)
                sent[7][:, cols] = jnp.where(own_rows == 0, terms[:BLK], terms[BLK:])
            sent.start(6)
            sent.start(7)
        put_terms(3, [stay[...], leave[...]], [tokens_here[0::2], tokens_here[1::2]])

    (queries_t, keys_t, values_t, keys, values, _, query_grad_t, key_acc, value_acc) = first
    sums = (pair, slice(0, blocks), slice(0, BLK), slice(0, BLK))
    operands = [(part, (own, slice(0, step))) for part in far_grads_t]
    operands += [(queries_t, half_across), (keys_t, across), (values_t, across)]
    operands += [(keys, down), (values, down), (key_acc, sums), (value_acc, sums)]
    operands += [(query_grad_t, half_across)]
    operands += whole([*tokens, *grads, *attended])
    results = [((BLK, half), BF)] + [((half, 3 * BLK), BF)] * 2
    results += [((3 * BLK, model // 2), BF), ((3 * BLK, model // 2), F32)]
    if final:
        results += [((half - step, model), F32)]
        operands += whole([part for both in before for part in both])
        operands += whole([mate_rows, rows])
    if last:
        results += [((BLK, model), BF), ((BLK, model), F32)]
    scratch = [pltpu.VMEM((BLK, half), BF)] + [pltpu.VMEM((3 * BLK, half), BF)] * 2
    return run(body, "later_half", [plan, offsets.reshape(-1)], operands, results, scratch, 8)


def halves(pieces, low):
    kept = {place: part for place, part in pieces.items() if (place // low) % 2 == 0}
    return side_by_side([pieces[place + low].astype(BF) for place in kept]), kept


def joined(kept, came):
    block = came.shape[1] // len(kept)
    return {
        place: part + came[:, at * block : (at + 1) * block].astype(F32)
        for at, (place, part) in enumerate(kept.items())
    }


def tied(values, others):
    return list(lax.optimization_barrier((*values, *others))[: len(values)])


def phase(*values):
    flat, tree = jax.tree.flatten(values)
    return jax.tree.unflatten(tree, lax.optimization_barrier(tuple(flat)))


def to_owner(block_sum):
    seq_count, batch_count = lax.axis_size("seq"), lax.axis_size("batch")
    ratio = batch_count // seq_count
    moves = [
        (s * batch_count + b, (b // ratio) * batch_count + s * ratio + b % ratio)
        for s in range(seq_count)
        for b in range(batch_count)
    ]
    return lax.ppermute(block_sum, ("seq", "batch"), moves)


def per_device(hidden, grad_out, block_offsets, w_query, w_key, w_value, w_out):
    tokens = hidden[0]
    grad_rows = grad_out[0]
    offsets = block_offsets[0]
    row_count, width = tokens.shape
    seq_count = lax.axis_size("seq")
    batch_count = lax.axis_size("batch")
    seq_at = lax.axis_index("seq")
    head_width = width // seq_count
    head_size = head_width // offsets.shape[0]
    pairs = head_width // BLK
    half_count = seq_count // 2

    weights = (w_query, w_key, w_value)
    rows = weight_rows(seq_at, head_width, weights)
    shard_blocks = row_count // BLK
    blocks = shard_blocks * seq_count
    block_at = jnp.arange(blocks, dtype=jnp.int32)
    place_of = ((block_at // shard_blocks) ^ seq_at) * shard_blocks + block_at % shard_blocks
    col_block = width // batch_count
    direct = col_block == BLK
    col_order = jnp.arange(width // BLK, dtype=jnp.int32)
    if direct:
        half_at = jnp.arange(batch_count // 2, dtype=jnp.int32) * 2
        col_order = lax.axis_index("batch") ^ jnp.concatenate([half_at + 1, half_at])
    seq_rows = (seq_at ^ jnp.asarray([0, *range(half_count, seq_count)])) * head_width
    batch_at = lax.axis_index("batch")
    ratio = batch_count // seq_count
    out_order = jnp.concatenate(
        [(batch_at // ratio) ^ jnp.arange(seq_count), jnp.reshape(batch_at % ratio, (1,))]
    )
    plan = jnp.concatenate([place_of, seq_rows, col_order, out_order])
    order_at = blocks + 1 + half_count
    plan = plan.astype(jnp.int32)

    mate_rows = weight_rows(seq_at ^ 1, head_width, weights)
    near_tokens = spread(tokens, "seq", half_count)
    near_grads = spread(grad_rows, "seq", half_count)
    projected = project(
        plan, blocks, near_tokens, near_grads, rows, w_out, 1.0 / math.sqrt(head_size)
    )
    projected, far_grads_t, (early, late) = projected[:6], projected[6:-2], projected[-2:]
    far_tokens = swap(tokens, "seq", half_count)
    plan, flat_offsets = plan, offsets.reshape(-1)
    far_tokens, mate_rows, projected, far_grads_t, early, late, plan, flat_offsets = phase(
        far_tokens, mate_rows, projected, far_grads_t, early, late, plan, flat_offsets
    )
    offsets = flat_offsets.reshape(offsets.shape)
    far_grads_t = [swap(part, "seq", half_count + at) for at, part in enumerate(far_grads_t)]
    early = swap(early, "seq", half_count)
    far_tokens = spread(far_tokens, "seq", half_count)
    first = own_half(plan, offsets, far_tokens, rows, projected)
    first, far_grads_t, early, late = phase(first, far_grads_t, early, late)
    late = swap(late, "seq", half_count)
    early = spread(early, "seq", half_count)
    all_tokens = near_tokens + far_tokens

    even = range(0, batch_count, 2)

    def begin(sent_terms, kept_terms):
        if direct:
            return sent_terms, {p: kept_terms[:, p // 2 * BLK : (p // 2 + 1) * BLK] for p in even}
        terms = jnp.concatenate([sent_terms.astype(F32), kept_terms], axis=1)
        pieces = [
            lax.dynamic_slice(
                terms, (0, (batch_at ^ p) * col_block), (terms.shape[0], col_block)
            )
            for p in range(batch_count)
        ]
        return side_by_side([pieces[p + 1].astype(BF) for p in even]), {p: pieces[p] for p in even}

    def begin_out(attended, terms):
        if direct and ratio == pairs:
            return terms[0], {p: terms[1][:, p // 2 * head_width : (p // 2 + 1) * head_width] for p in even}
        attended_t = jnp.concatenate([first[5], jnp.concatenate(attended, axis=0)], axis=1)
        grads = jnp.concatenate(all_grads, axis=0)
        terms = jnp.dot(attended_t, grads, preferred_element_type=F32)
        height = head_width // ratio
        pieces = []
        for p in range(batch_count):
            target = batch_at ^ p
            corner = ((target % ratio) * height, (target // ratio) * head_width)
            pieces.append(lax.dynamic_slice(terms, corner, (height, head_width)))
        return side_by_side([pieces[p + 1].astype(BF) for p in even]), {p: pieces[p] for p in even}

    kept, came_terms, stayed, came, attended = [], [], [], [], []
    for pair in range(pairs):
        last = pair == pairs - 1
        all_grads = []
        if last:
            late = spread(late, "seq", half_count)
            late, came = phase(late, came)
            all_grads = near_grads + [part for both in zip(early, late) for part in both]
        far_attended, stay, leave, *terms = later_half(
            plan,
            offsets,
            order_at,
            far_grads_t,
            pair,
            first,
            all_tokens,
            all_grads if direct and ratio == pairs else [],
            [first[5], *attended] if last and direct and ratio == pairs else [],
            list(zip(stayed, came)),
            rows if last else None,
            mate_rows,
        )
        if last:
            stay, leave, terms, came_terms = phase(stay, leave, terms, came_terms)
        else:
            stay, leave, terms, far_attended, early, late, first = phase(
                stay, leave, terms, far_attended, early, late, first
            )
        attended.append(far_attended)
        stayed.append(stay)
        came.append(swap(leave, "seq", 1))
        if not last:
            goes, kept_head = begin(*terms)
            kept.append(kept_head)
            came_terms.append(swap(goes, "batch", 1))

    levels = [1 << bit for bit in range(1, batch_count.bit_length() - 1)]
    goes, kept_out = begin_out(attended, terms[3:])
    came_out = swap(goes, "batch", 1)
    goes_head, kept_head = begin(*terms[:2])
    pieces = [None] * len(kept)
    lags = [1] * len(pieces)

    def start(at, turn):
        goes, kept = halves(pieces[at], levels[turn - lags[at]])
        return at, kept, swap(goes, "batch", levels[turn - lags[at]])

    def due(turn):
        return [at for at in range(len(pieces)) if 0 <= turn - lags[at] < len(levels)]

    moving = []

    held = [rows, mate_rows]
    sent = []
    for at in range(1, half_count):
        mate = came[-1][at * row_count : (at + 1) * row_count]
        total = jnp.dot(mate, mate_rows[(pairs - 1) * 3 * BLK :], preferred_element_type=F32)
        total += terms[2][(at - 1) * row_count : at * row_count]
        sent.append(total.astype(BF))
    cut = row_count // 2
    sent = [(part[:cut], part[cut:]) for part in sent]
    stayed, came, sent_after = phase(stayed, came, sent)
    partial = 0.0
    for pair in range(pairs):
        for side, parts in enumerate((stayed, came)):
            weight = held[side][pair * 3 * BLK : (pair + 1) * 3 * BLK]
            partial += jnp.dot(parts[pair][:row_count], weight, preferred_element_type=F32)
    token_parts = [swap(part[0], "seq", 2 * at) for at, part in enumerate(sent, 1)]
    came_head = swap(goes_head, "batch", 1)

    turn, out_part = 0, None
    while turn < 2 + len(levels):
        transfers = [came for _, _, came in moving]
        if turn == 0:
            came_terms, came_out, sent_after = phase(came_terms, came_out, sent_after)
            pieces = [joined(*both) for both in zip(kept, came_terms)]
            later_parts = [swap(part[1], "seq", 2 * at) for at, part in enumerate(sent_after, 1)]
            pieces.append(joined(kept_out, came_out))
            lags.append(1)
        elif turn == 1:
            transfers, came_head, token_parts = phase(transfers, came_head, token_parts)
            pieces.append(joined(kept_head, came_head))
            lags.append(2)
        elif turn == 2:
            transfers, later_parts = phase(transfers, later_parts)
        else:
            transfers = phase(transfers)[0]
        for (at, kept_now, _), came_now in zip(moving, transfers):
            pieces[at] = joined(kept_now, came_now)
        turn += 1
        moving = [start(at, turn) for at in due(turn)]
        if turn == 1 + len(levels):
            out_part = to_owner(pieces[pairs - 1][0])[None]

    grad_hidden = partial
    for both in zip(token_parts, later_parts):
        grad_hidden = grad_hidden + jnp.concatenate(both, axis=0).astype(F32)
    grad_hidden = grad_hidden.astype(BF)
    head_sums = [pieces[at][0] for at in range(len(pieces)) if at != pairs - 1]
    row_block = width // batch_count
    head_part = jnp.stack([part.reshape(3, BLK, row_block) for part in head_sums], axis=1)
    head_part = head_part.reshape(3, head_width, row_block).transpose(0, 2, 1)
    grad_weights = jnp.concatenate([head_part, out_part], axis=0)
    norm_factor = 1.0 / math.sqrt(row_count * seq_count * batch_count)
    return (grad_hidden[None], grad_weights * norm_factor)


def solution(mesh):
    placed = (
        P("batch", "seq", None),
        P("batch", "seq", None),
        P("batch", "seq", None, None),
        P(),
        P(),
        P(),
        P(),
    )
    return jax.shard_map(
        per_device,
        mesh=mesh,
        in_specs=placed,
        out_specs=(P("batch", "seq", None), P(None, "batch", "seq")),
        check_vma=False,
    )
```

```python
import functools
import math

import jax
import jax.numpy as jnp
from jax import lax
from jax.experimental import pallas as pl
from jax.experimental.pallas import tpu as pltpu
from jax.sharding import PartitionSpec as P

BLK = 128
BF = jnp.bfloat16
F32 = jnp.float32
LAST_LAST = (((1,), (1,)), ((), ()))
VMEM_BYTES = 66584576
LIGHT = pl.CostEstimate(flops=1, bytes_accessed=1, transcendentals=0)


def dot(left_side, right_side, dims):
    return lax.dot_general(left_side, right_side, dims, preferred_element_type=F32)


def swap(value, axis, distance):
    count = lax.axis_size(axis)
    return lax.ppermute(value, axis, [(at, at ^ distance) for at in range(count)])


def spread(shard, axis, count):
    pieces = {0: shard}
    bit = count // 2
    while bit:
        for place in sorted(pieces):
            pieces[place | bit] = swap(pieces[place], axis, bit)
        bit //= 2
    return [pieces[place] for place in sorted(pieces)]


def side_by_side(parts):
    return parts[0] if len(parts) == 1 else jnp.concatenate(parts, axis=1)


class Held:
    def __init__(self, source, target, arrived):
        self.target, self.copy, self.there = target, None, False
        self.copy = pltpu.make_async_copy(source, target, arrived)
        self.copy.start()

    def __call__(self):
        if not self.there:
            self.copy.wait()
            self.there = True
        return self.target


class Sent:
    def __init__(self, outs, held, left):
        self.outs, self.held, self.left, self.copies = outs, held, left, []

    def __getitem__(self, at):
        return self.held[at]

    def start(self, at, part=None):
        source, target = self.held[at], self.outs[at]
        if part is not None:
            source, target = source.at[part], target.at[part]
        copy = pltpu.make_async_copy(source, target, self.left.at[len(self.copies)])
        copy.start()
        self.copies.append(copy)

    def finish(self):
        for copy in self.copies:
            copy.wait()


def part_shape(shape, part):
    if part is None:
        return shape
    kept = []
    for size, index in zip(shape, part):
        if isinstance(index, slice):
            kept.append(len(range(*index.indices(size))))
        elif not isinstance(index, int):
            kept.append(index.size)
    return tuple(kept)


def run(body, name, scalars, operands, results, scratch, most_copies):
    arrays = [array for array, _ in operands]
    taken = [
        part_shape(array.shape, part([None] * 99, 0) if callable(part) else part)
        for array, part in operands
    ]
    n, k, m = len(scalars), len(arrays), len(results)

    def kernel(*refs):
        given, sources, outs = refs[:n], refs[n : n + k], refs[n + k : n + k + m]
        refs = refs[n + k + m :]
        targets, held, own, (arrived, left) = refs[:k], refs[k : k + m], refs[k + m : -2], refs[-2:]
        ready = []
        for at, (source, (_, part)) in enumerate(zip(sources, operands)):
            if callable(part):
                part = part(given, None)
            source = source if part is None else source.at[part]
            ready.append(Held(source, targets[at], arrived.at[at]))
        sent = Sent(outs, held, left)
        body(given, ready, sent, *own)
        sent.finish()

    return pl.pallas_call(
        kernel,
        in_specs=[pl.BlockSpec(memory_space=pltpu.SMEM)] * n + [pl.BlockSpec(memory_space=pl.ANY)] * k,
        out_specs=[pl.BlockSpec(memory_space=pl.ANY)] * m,
        out_shape=[jax.ShapeDtypeStruct(*result) for result in results],
        scratch_shapes=[pltpu.VMEM(shape, array.dtype) for shape, array in zip(taken, arrays)]
        + [pltpu.VMEM(*result) for result in results]
        + scratch
        + [pltpu.SemaphoreType.DMA((k,)), pltpu.SemaphoreType.DMA((most_copies,))],
        compiler_params=pltpu.CompilerParams(vmem_limit_bytes=VMEM_BYTES),
        cost_estimate=LIGHT,
        name=name,
    )(*scalars, *arrays)


def whole(arrays):
    return [(array, None) for array in arrays]


def weight_rows(seq_index, head_width, weights):
    width, count = weights[0].shape[0], len(weights)
    pairs = head_width // BLK
    first = jnp.reshape(seq_index * head_width, (1,)).astype(jnp.int32)

    def cols(scalars, dry):
        start = 0 if dry is not None else pl.multiple_of(scalars[0][0], BLK)
        return (slice(0, width), pl.ds(start, head_width))

    def body(_, ready, sent):
        rows = sent[0]
        for at in range(count):
            taken = ready[at]()
            for pair in range(pairs):
                base = (pair * count + at) * BLK
                rows[base : base + BLK, :] = taken[:, pair * BLK : (pair + 1) * BLK].T
        sent.start(0)

    operands = [(weight, cols) for weight in weights]
    return run(body, "weight_rows", [first], operands, [((count * head_width, width), BF)], [], 1)[0]


def out_rows_part(blocks, more, height, model):
    def part(scalars, dry):
        start = 0 if dry is not None else pl.multiple_of(scalars[0][blocks] + more, BLK)
        return (pl.ds(start, height), slice(0, model))

    return part


def project(plan, blocks, tokens, grads, rows, out_weight, scale):
    count, (step, model) = len(tokens), tokens[0].shape
    width = rows.shape[0] // 3
    pairs = width // BLK
    across, down = ((width, count * step), BF), ((count * step, width), BF)

    def body(_, ready, sent):
        rows, out_rows, far_rows = ready[0], ready[1], ready[2 : 2 + count]
        tokens_here, grads_here = ready[2 + count : 2 + 2 * count], ready[2 + 2 * count :]
        queries_t, out_grads_t, keys_t, values_t, keys, values = (sent[at] for at in range(6))
        own_grads = grads_here[0]()[...]
        for at in range(count):
            sent[6 + at][...] = dot(far_rows[at]()[...], own_grads, LAST_LAST).astype(BF)
            sent.start(6 + at)
        for at in range(2):
            sent[6 + count + at][...] = own_grads[at * step // 2 : (at + 1) * step // 2]
            sent.start(6 + count + at)
        for at in range(count):
            span = slice(at * step, (at + 1) * step)
            heads_t = dot(rows()[...], tokens_here[at]()[...], LAST_LAST)
            for pair in range(pairs):
                own = slice(pair * BLK, (pair + 1) * BLK)
                base = pair * 3 * BLK
                queries_t[own, span] = heads_t[base : base + BLK].astype(BF) * scale
                key_part = heads_t[base + BLK : base + 2 * BLK]
                value_part = heads_t[base + 2 * BLK : base + 3 * BLK]
                keys_t[own, span] = key_part.astype(BF)
                values_t[own, span] = value_part.astype(BF)
                keys[span, own] = key_part.T.astype(BF)
                values[span, own] = value_part.T.astype(BF)
        for at in (0, 2, 3, 4, 5):
            sent.start(at)
        for at in range(count):
            span = slice(at * step, (at + 1) * step)
            out_grads_t[:, span] = dot(out_rows()[...], grads_here[at]()[...], LAST_LAST).astype(BF)
        sent.start(1)

    operands = [(rows, None), (out_weight, out_rows_part(blocks, 0, width, model))]
    operands += [
        (out_weight, out_rows_part(blocks + 1 + at, 0, width, model)) for at in range(count)
    ]
    operands += whole(tokens) + whole(grads)
    results = [across] * 4 + [down] * 2 + [((width, step), BF)] * count
    results += [((step // 2, model), BF)] * 2
    return run(body, "project", [plan], operands, results, [], 8 + count)


def attend(
    place_of, offsets, head_base, places, queries_t, out_grads_t, key_refs, sums, put, slots, blocks, head_size
):
    keys_t, values_t, keys, values = key_refs
    key_at = lax.broadcasted_iota(jnp.int32, (BLK, BLK), 0)
    query_at = lax.broadcasted_iota(jnp.int32, (BLK, BLK), 1)
    causal = key_at <= query_at
    first_head = lax.broadcasted_iota(jnp.int32, (2 * head_size, BLK), 0) < head_size
    plus = functools.partial(functools.reduce, jnp.add)
    cut = [slice(slot * BLK, (slot + 1) * BLK) for slot in range(slots)]

    for step in range(queries_t.shape[1] // BLK):
        place = places + step
        block = place_of[place]
        cols = slice(step * BLK, (step + 1) * BLK)
        pair_queries = queries_t[:, cols]
        pair_grads = out_grads_t[:, cols]
        scored = []
        for half in range(2):
            head = head_base + half
            rows = slice(half * head_size, (half + 1) * head_size)
            keep = first_head if half == 0 else ~first_head
            head_queries = jnp.where(keep, pair_queries, jnp.zeros_like(pair_queries))
            head_grads = jnp.where(keep, pair_grads, jnp.zeros_like(pair_grads))
            named, usable = [], []
            for slot in range(slots):
                offset = offsets[(head * blocks + block) * slots + slot]
                usable.append(offset <= block)
                named.append(place_of[jnp.where(offset <= block, block - offset, 0)])
            spans = [pl.ds(pl.multiple_of(at * BLK, BLK), BLK) for at in named]
            seen_keys = jnp.concatenate([keys[span, :] for span in spans], axis=0)
            seen_values = jnp.concatenate([values[span, :] for span in spans], axis=0)
            scores = jnp.dot(seen_keys, head_queries, preferred_element_type=F32)
            prob_grad = jnp.dot(seen_values, head_grads, preferred_element_type=F32)
            scores = [
                jnp.where(causal if slot == 0 else usable[slot], scores[cut[slot]], -jnp.inf)
                for slot in range(slots)
            ]
            scored.append((rows, named, spans, scores, [prob_grad[part] for part in cut]))
        parts = []
        for rows, named, spans, scores, prob_grad in scored:
            top = jnp.max(functools.reduce(jnp.maximum, scores), axis=0, keepdims=True)
            raised = [jnp.exp(part - top) for part in scores]
            total = jnp.sum(plus(raised), axis=0, keepdims=True)
            inverse = 1.0 / total
            probs = [part * inverse for part in raised]
            probs_half = jnp.concatenate([part.astype(BF) for part in probs], axis=0)
            delta = jnp.sum(
                plus([part * grad for part, grad in zip(probs, prob_grad)]), axis=0, keepdims=True
            )
            score_grad = jnp.concatenate(
                [(part * (grad - delta)).astype(BF) for part, grad in zip(probs, prob_grad)], axis=0
            )
            seen_values_t = side_by_side([values_t[rows, span] for span in spans])
            seen_keys_t = side_by_side([keys_t[rows, span] for span in spans])
            attended = jnp.dot(seen_values_t, probs_half, preferred_element_type=F32)
            query_grad = jnp.dot(seen_keys_t, score_grad, preferred_element_type=F32)
            put(rows, cols, attended, query_grad * (1.0 / math.sqrt(head_size)))
            value_part = dot(out_grads_t[rows, cols], probs_half, LAST_LAST)
            key_part = dot(queries_t[rows, cols], score_grad, LAST_LAST)
            parts.append((rows, named, key_part, value_part))
        key_acc, value_acc = sums()
        for rows, named, key_part, value_part in parts:
            for at, part in zip(named, cut):
                key_acc[at, rows, :] += key_part[:, part]
                value_acc[at, rows, :] += value_part[:, part]


def own_half(plan, offsets, tokens, rows, projected):
    width, half = projected[0].shape
    heads, blocks, slots = offsets.shape
    head_size, pairs, total, count = width // heads, width // BLK, blocks * BLK, len(tokens)
    half_across, across, down = ((width, half), BF), ((width, total), BF), ((total, width), BF)
    sums = ((pairs, blocks, BLK, BLK), F32)
    scale = 1.0 / math.sqrt(head_size)

    def body(scalars, ready, sent):
        rows, tokens_here = ready[0], ready[1 : 1 + count]
        queries_t, out_grads_t, keys_in, values_in, keys_down, values_down = ready[1 + count :]
        later_queries_t, keys_t, values_t, keys, values = (sent[at] for at in range(5))
        attended_t, query_grad_t, key_acc, value_acc = (sent[at] for at in range(5, 9))
        key_acc[...] = jnp.zeros(key_acc.shape, F32)
        value_acc[...] = jnp.zeros(value_acc.shape, F32)
        step = tokens[0].shape[0]
        for at in range(count):
            span = slice(at * step, (at + 1) * step)
            placed = slice(half + at * step, half + (at + 1) * step)
            for pair in range(pairs):
                own = slice(pair * BLK, (pair + 1) * BLK)
                pair_rows = rows()[pair * 3 * BLK : (pair + 1) * 3 * BLK, :]
                heads_t = dot(pair_rows, tokens_here[at]()[...], LAST_LAST)
                later_queries_t[own, span] = heads_t[:BLK].astype(BF) * scale
                keys_t[own, placed] = heads_t[BLK : 2 * BLK].astype(BF)
                values_t[own, placed] = heads_t[2 * BLK :].astype(BF)
                keys[placed, own] = heads_t[BLK : 2 * BLK].T.astype(BF)
                values[placed, own] = heads_t[2 * BLK :].T.astype(BF)
        keys_t[:, :half] = keys_in()[...]
        values_t[:, :half] = values_in()[...]
        keys[:half, :] = keys_down()[...]
        values[:half, :] = values_down()[...]
        for at in range(5):
            sent.start(at)

        for pair in range(pairs):
            own = slice(pair * BLK, (pair + 1) * BLK)

            def put(at_rows, cols, attended, query_grad):
                placed = slice(own.start + at_rows.start, own.start + at_rows.stop)
                attended_t[placed, cols] = attended.astype(BF)
                query_grad_t[placed, cols] = query_grad.astype(BF)

            attend(
                scalars[0],
                scalars[1],
                2 * pair,
                0,
                queries_t().at[own, :],
                out_grads_t().at[own, :],
                (keys_t.at[own, :], values_t.at[own, :], keys.at[:, own], values.at[:, own]),
                lambda pair=pair: (key_acc.at[pair], value_acc.at[pair]),
                put,
                slots,
                blocks,
                head_size,
            )
            for at in (5, 6):
                sent.start(at, (own, slice(0, half)))
            for at in (7, 8):
                sent.start(at, (pair,))

    results = [half_across, across, across, down, down, half_across, half_across, sums, sums]
    operands = whole([rows, *tokens, *projected])
    return run(
        body, "own_half", [plan, offsets.reshape(-1)], operands, results, [], 5 + 4 * pairs
    )


def later_half(
    plan, offsets, order_at, far_grads_t, pair, first, tokens, grads, attended, before, rows, mate_rows
):
    width, half = first[0].shape
    heads, blocks, slots = offsets.shape
    head_size, total = width // heads, blocks * BLK
    near, step = len(far_grads_t), far_grads_t[0].shape[1]
    model, count = tokens[0].shape[1], len(tokens)
    own = slice(pair * BLK, (pair + 1) * BLK)
    across, half_across, down = (own, slice(0, total)), (own, slice(0, half)), (slice(0, total), own)
    last, final = bool(grads), rows is not None

    def body(scalars, ready, sent, out_grads_t, stay, leave):
        plan = scalars[0]
        queries_t, keys_t, values_t, keys, values = (part() for part in ready[near : near + 5])
        query_grad_first = ready[near + 7]
        tokens_here = ready[near + 8 : near + 8 + count]
        grads_here = ready[near + 8 + count : near + 8 + count + len(grads)]
        attended_here = ready[near + 8 + count + len(grads) :]
        attended_here, shares_here = attended_here[: len(attended)], attended_here[len(attended) :]
        attended_t = sent[0]
        for at in range(near):
            out_grads_t[:, at * step : (at + 1) * step] = ready[at]()[...]

        def columns(place, at):
            left = place // 2 * step + at
            return (leave if place % 2 else stay), slice(left, left + BLK)

        def put(at_rows, cols, attended, query_grad):
            attended_t[at_rows, cols] = attended.astype(BF)
            target, placed = columns(near + cols.start // step, cols.start % step)
            target[at_rows, placed] = query_grad.astype(BF)

        attend(
            plan,
            scalars[1],
            2 * pair,
            blocks // 2,
            queries_t,
            out_grads_t,
            (keys_t, values_t, keys, values),
            lambda: (ready[near + 5](), ready[near + 6]()),
            put,
            slots,
            blocks,
            head_size,
        )
        if not last:
            sent.start(0)
        for at in range(0, half, BLK):
            target, cols = columns(at // step, at % step)
            target[:BLK, cols] = query_grad_first()[:, at : at + BLK]
        key_acc, value_acc = ready[near + 5](), ready[near + 6]()
        for at in range(blocks):
            target, cols = columns(at * BLK // step, at * BLK % step)
            target[BLK : 2 * BLK, cols] = key_acc[at].astype(BF)
            target[2 * BLK :, cols] = value_acc[at].astype(BF)
        for at, held in ((1, stay), (2, leave)):
            for cols in range(0, half, BLK):
                sent[at][cols : cols + BLK, :] = held[:, cols : cols + BLK].T
            sent.start(at)
        if final:
            parts = [(sent[1], shares_here[-1], pair)]
            parts += [
                (shares_here[2 * at + side], shares_here[-1 - side], at)
                for at in range(len(before))
                for side in (1, 0)
            ]
            lefts = [left()[...] if isinstance(left, Held) else left[step:, :] for left, _, _ in parts]
            left = jnp.concatenate(lefts, axis=1)
            model_n = rows.shape[1]
            for col in range(0, model_n, 2 * BLK):
                cols = slice(col, col + 2 * BLK)
                held = [
                    right()[at * 3 * BLK : (at + 1) * 3 * BLK, cols] for _, right, at in parts
                ]
                sent[5][:, cols] = jnp.dot(
                    left, jnp.concatenate(held, axis=0), preferred_element_type=F32
                )
            sent.start(5)

        def put_terms(at, lefts, rights):
            pieces = [[part() for part in right] for right in rights]
            for col in range(0, model, 2 * BLK):
                spans = [
                    pl.ds(pl.multiple_of(plan[order_at + col // BLK + side] * BLK, BLK), BLK)
                    for side in range(2)
                ]
                terms = 0.0
                for left, right in zip(lefts, pieces):
                    cut = [side_by_side([part[:, span] for span in spans]) for part in right]
                    terms += jnp.dot(
                        left, jnp.concatenate(cut, axis=0), preferred_element_type=F32
                    )
                target, cols = sent[at + col // (model // 2)], col % (model // 2)
                target[:, cols : cols + 2 * BLK] = terms.astype(target.dtype)
                if cols + 2 * BLK == model // 2:
                    sent.start(at + col // (model // 2))

        if last:
            lefts = [attended_here[0]()[...]]
            lefts.append(
                jnp.concatenate([part()[...] for part in attended_here[1:]] + [attended_t[...]], axis=0)
            )
            pieces = [[part() for part in grads_here[:near]], [part() for part in grads_here[near:]]]
            own_rows = plan[order_at + model // BLK + model // width]
            for at in range(model // width):
                span = pl.ds(
                    pl.multiple_of(plan[order_at + model // BLK + at] * width, width), width
                )
                terms = 0.0
                for left, right in zip(lefts, pieces):
                    taken = jnp.concatenate([part[:, span] for part in right], axis=0)
                    terms += jnp.dot(left, taken, preferred_element_type=F32)
                goes = jnp.where(own_rows == 0, terms[BLK:], terms[:BLK]).astype(BF)
                stays = jnp.where(own_rows == 0, terms[:BLK], terms[BLK:])
                cols = slice(at * BLK, (at + 1) * BLK)
                for side in range(width // BLK):
                    held = slice(side * BLK, (side + 1) * BLK)
                    sent[6][held, cols] = goes[:, held]
                    sent[7][held, cols] = stays[:, held]
            sent.start(6)
            sent.start(7)
        put_terms(3, [stay[...], leave[...]], [tokens_here[0::2], tokens_here[1::2]])

    (queries_t, keys_t, values_t, keys, values, _, query_grad_t, key_acc, value_acc) = first
    sums = (pair, slice(0, blocks), slice(0, BLK), slice(0, BLK))
    operands = [(part, (own, slice(0, step))) for part in far_grads_t]
    operands += [(queries_t, half_across), (keys_t, across), (values_t, across)]
    operands += [(keys, down), (values, down), (key_acc, sums), (value_acc, sums)]
    operands += [(query_grad_t, half_across)]
    operands += whole([*tokens, *grads, *attended])
    results = [((BLK, half), BF)] + [((half, 3 * BLK), BF)] * 2
    results += [((3 * BLK, model // 2), BF), ((3 * BLK, model // 2), F32)]
    if final:
        results += [((half - step, model), F32)]
        far_places = (slice(step, half), slice(0, 3 * BLK))
        operands += [(part, far_places) for both in before for part in both]
        if before:
            operands += [(mate_rows, (slice(0, len(before) * 3 * BLK), slice(0, model)))]
        operands += [(rows, None)]
    if last:
        results += [((width, model // 2), BF), ((width, model // 2), F32)]
    scratch = [pltpu.VMEM((BLK, half), BF)] + [pltpu.VMEM((3 * BLK, half), BF)] * 2
    return run(body, "later_half", [plan, offsets.reshape(-1)], operands, results, scratch, 8)


def halves(pieces, low):
    kept = {place: part for place, part in pieces.items() if (place // low) % 2 == 0}
    return side_by_side([pieces[place + low].astype(BF) for place in kept]), kept


def joined(kept, came):
    block = came.shape[1] // len(kept)
    return {
        place: part + came[:, at * block : (at + 1) * block].astype(F32)
        for at, (place, part) in enumerate(kept.items())
    }


def tied(values, others):
    return list(lax.optimization_barrier((*values, *others))[: len(values)])


def phase(*values):
    flat, tree = jax.tree.flatten(values)
    return jax.tree.unflatten(tree, lax.optimization_barrier(tuple(flat)))


def to_owner(block_sum):
    seq_count, batch_count = lax.axis_size("seq"), lax.axis_size("batch")
    ratio = batch_count // seq_count
    moves = [
        (s * batch_count + b, (b // ratio) * batch_count + s * ratio + b % ratio)
        for s in range(seq_count)
        for b in range(batch_count)
    ]
    return lax.ppermute(block_sum, ("seq", "batch"), moves)


def per_device(hidden, grad_out, block_offsets, w_query, w_key, w_value, w_out):
    tokens = hidden[0]
    grad_rows = grad_out[0]
    offsets = block_offsets[0]
    row_count, width = tokens.shape
    seq_count = lax.axis_size("seq")
    batch_count = lax.axis_size("batch")
    seq_at = lax.axis_index("seq")
    head_width = width // seq_count
    head_size = head_width // offsets.shape[0]
    pairs = head_width // BLK
    half_count = seq_count // 2

    weights = (w_query, w_key, w_value)
    rows = weight_rows(seq_at, head_width, weights)
    shard_blocks = row_count // BLK
    blocks = shard_blocks * seq_count
    block_at = jnp.arange(blocks, dtype=jnp.int32)
    place_of = ((block_at // shard_blocks) ^ seq_at) * shard_blocks + block_at % shard_blocks
    col_block = width // batch_count
    direct = col_block == BLK
    col_order = jnp.arange(width // BLK, dtype=jnp.int32)
    if direct:
        half_at = jnp.arange(batch_count // 2, dtype=jnp.int32) * 2
        col_order = lax.axis_index("batch") ^ jnp.concatenate([half_at + 1, half_at])
    seq_rows = (seq_at ^ jnp.asarray([0, *range(half_count, seq_count)])) * head_width
    batch_at = lax.axis_index("batch")
    ratio = batch_count // seq_count
    out_order = jnp.concatenate(
        [(batch_at // ratio) ^ jnp.arange(seq_count), jnp.reshape(batch_at % ratio, (1,))]
    )
    plan = jnp.concatenate([place_of, seq_rows, col_order, out_order])
    order_at = blocks + 1 + half_count
    plan = plan.astype(jnp.int32)

    mate_rows = weight_rows(seq_at ^ 1, head_width, weights)
    near_tokens = spread(tokens, "seq", half_count)
    near_grads = spread(grad_rows, "seq", half_count)
    projected = project(
        plan, blocks, near_tokens, near_grads, rows, w_out, 1.0 / math.sqrt(head_size)
    )
    projected, far_grads_t, (early, late) = projected[:6], projected[6:-2], projected[-2:]
    far_tokens = swap(tokens, "seq", half_count)
    plan, flat_offsets = plan, offsets.reshape(-1)
    far_tokens, mate_rows, projected, far_grads_t, early, late, plan, flat_offsets = phase(
        far_tokens, mate_rows, projected, far_grads_t, early, late, plan, flat_offsets
    )
    offsets = flat_offsets.reshape(offsets.shape)
    far_grads_t = [swap(part, "seq", half_count + at) for at, part in enumerate(far_grads_t)]
    early = swap(early, "seq", half_count)
    far_tokens = spread(far_tokens, "seq", half_count)
    first = own_half(plan, offsets, far_tokens, rows, projected)
    first, far_grads_t, early, late = phase(first, far_grads_t, early, late)
    late = swap(late, "seq", half_count)
    early = spread(early, "seq", half_count)
    all_tokens = near_tokens + far_tokens

    even = range(0, batch_count, 2)

    def begin(sent_terms, kept_terms):
        if direct:
            return sent_terms, {p: kept_terms[:, p // 2 * BLK : (p // 2 + 1) * BLK] for p in even}
        terms = jnp.concatenate([sent_terms.astype(F32), kept_terms], axis=1)
        pieces = [
            lax.dynamic_slice(
                terms, (0, (batch_at ^ p) * col_block), (terms.shape[0], col_block)
            )
            for p in range(batch_count)
        ]
        return side_by_side([pieces[p + 1].astype(BF) for p in even]), {p: pieces[p] for p in even}

    def begin_out(attended, terms):
        if direct and ratio == pairs:
            return begin(*terms)
        attended_t = jnp.concatenate([first[5], jnp.concatenate(attended, axis=0)], axis=1)
        grads = jnp.concatenate(all_grads, axis=0)
        terms = jnp.dot(attended_t, grads, preferred_element_type=F32)
        height = head_width // ratio
        pieces = []
        for p in range(batch_count):
            target = batch_at ^ p
            corner = ((target % ratio) * height, (target // ratio) * head_width)
            pieces.append(lax.dynamic_slice(terms, corner, (height, head_width)))
        return side_by_side([pieces[p + 1].astype(BF) for p in even]), {p: pieces[p] for p in even}

    kept, came_terms, stayed, came, attended = [], [], [], [], []
    for pair in range(pairs):
        last = pair == pairs - 1
        all_grads = []
        if last:
            late = spread(late, "seq", half_count)
            late, came = phase(late, came)
            all_grads = near_grads + [part for both in zip(early, late) for part in both]
        far_attended, stay, leave, *terms = later_half(
            plan,
            offsets,
            order_at,
            far_grads_t,
            pair,
            first,
            all_tokens,
            all_grads if direct and ratio == pairs else [],
            [first[5], *attended] if last and direct and ratio == pairs else [],
            list(zip(stayed, came)),
            rows if last else None,
            mate_rows,
        )
        if last:
            stay, leave, terms, came_terms = phase(stay, leave, terms, came_terms)
        else:
            stay, leave, terms, far_attended, early, late, first = phase(
                stay, leave, terms, far_attended, early, late, first
            )
        attended.append(far_attended)
        stayed.append(stay)
        came.append(swap(leave, "seq", 1))
        if not last:
            goes, kept_head = begin(*terms)
            kept.append(kept_head)
            came_terms.append(swap(goes, "batch", 1))

    levels = [1 << bit for bit in range(1, batch_count.bit_length() - 1)]
    goes, kept_out = begin_out(attended, terms[3:])
    came_out = swap(goes, "batch", 1)
    goes_head, kept_head = begin(*terms[:2])
    pieces = [None] * len(kept)
    lags = []

    def start(at, turn):
        goes, kept = halves(pieces[at], levels[turn - lags[at]])
        return at, kept, swap(goes, "batch", levels[turn - lags[at]])

    def due(turn):
        return [at for at in range(len(pieces)) if 0 <= turn - lags[at] < len(levels)]

    moving = []

    held = [rows, mate_rows]
    sent = []
    for at in range(1, half_count):
        mate = came[-1][at * row_count : (at + 1) * row_count]
        total = jnp.dot(mate, mate_rows[(pairs - 1) * 3 * BLK :], preferred_element_type=F32)
        total += terms[2][(at - 1) * row_count : at * row_count]
        sent.append(total.astype(BF))
    cut = row_count // 2
    sent = [(part[:cut], part[cut:]) for part in sent]
    stayed, came, sent_after = phase(stayed, came, sent)
    partial = 0.0
    for pair in range(pairs):
        for side, parts in enumerate((stayed, came)):
            weight = held[side][pair * 3 * BLK : (pair + 1) * 3 * BLK]
            partial += jnp.dot(parts[pair][:row_count], weight, preferred_element_type=F32)
    token_parts = [swap(part[0], "seq", 2 * at) for at, part in enumerate(sent, 1)]
    came_head = swap(goes_head, "batch", 1)

    merged = direct and ratio == pairs
    turn, out_at = 0, 0 if merged else pairs - 1
    while turn < 2 + len(levels):
        transfers = [came for _, _, came in moving]
        if turn == 0:
            came_terms, came_out, sent_after = phase(came_terms, came_out, sent_after)
            pieces = [joined(*both) for both in zip(kept, came_terms)]
            pieces.append(joined(kept_out, came_out))
            if merged:
                pieces = [{p: jnp.concatenate([part[p] for part in pieces], axis=0) for p in even}]
            later_parts = [swap(part[1], "seq", 2 * at) for at, part in enumerate(sent_after, 1)]
            lags = [1] * len(pieces)
        elif turn == 1:
            transfers, came_head, token_parts = phase(transfers, came_head, token_parts)
            pieces.append(joined(kept_head, came_head))
            lags.append(2)
        elif turn == 2:
            transfers, later_parts = phase(transfers, later_parts)
        else:
            transfers = phase(transfers)[0]
        for (at, kept_now, _), came_now in zip(moving, transfers):
            pieces[at] = joined(kept_now, came_now)
        turn += 1
        moving = [start(at, turn) for at in due(turn)]
        if turn == 1 + len(levels):
            out_sum, head_sums = pieces[out_at][0], []
            if merged:
                top = 3 * BLK * (pairs - 1)
                head_sums = [out_sum[at : at + 3 * BLK] for at in range(0, top, 3 * BLK)]
                out_sum = side_by_side(
                    [out_sum[at : at + BLK] for at in range(top, top + head_width, BLK)]
                )
            out_part = to_owner(out_sum)[None]

    grad_hidden = partial
    for both in zip(token_parts, later_parts):
        grad_hidden = grad_hidden + jnp.concatenate(both, axis=0).astype(F32)
    grad_hidden = grad_hidden.astype(BF)
    head_sums += [pieces[at][0] for at in range(len(pieces)) if at != out_at]
    row_block = width // batch_count
    head_part = jnp.stack([part.reshape(3, BLK, row_block) for part in head_sums], axis=1)
    head_part = head_part.reshape(3, head_width, row_block).transpose(0, 2, 1)
    grad_weights = jnp.concatenate([head_part, out_part], axis=0)
    norm_factor = 1.0 / math.sqrt(row_count * seq_count * batch_count)
    return (grad_hidden[None], grad_weights * norm_factor)


def solution(mesh):
    placed = (
        P("batch", "seq", None),
        P("batch", "seq", None),
        P("batch", "seq", None, None),
        P(),
        P(),
        P(),
        P(),
    )
    return jax.shard_map(
        per_device,
        mesh=mesh,
        in_specs=placed,
        out_specs=(P("batch", "seq", None), P(None, "batch", "seq")),
        check_vma=False,
    )
```

```python
import functools
import math

import jax
import jax.numpy as jnp
from jax import lax
from jax.experimental import pallas as pl
from jax.experimental.pallas import tpu as pltpu
from jax.sharding import PartitionSpec as P

BLK = 128
BF = jnp.bfloat16
F32 = jnp.float32
LAST_LAST = (((1,), (1,)), ((), ()))
VMEM_BYTES = 66584576
LIGHT = pl.CostEstimate(flops=1, bytes_accessed=1, transcendentals=0)


def dot(left_side, right_side, dims):
    return lax.dot_general(left_side, right_side, dims, preferred_element_type=F32)


def swap(value, axis, distance):
    count = lax.axis_size(axis)
    return lax.ppermute(value, axis, [(at, at ^ distance) for at in range(count)])


def spread(shard, axis, count):
    pieces = {0: shard}
    bit = count // 2
    while bit:
        for place in sorted(pieces):
            pieces[place | bit] = swap(pieces[place], axis, bit)
        bit //= 2
    return [pieces[place] for place in sorted(pieces)]


def side_by_side(parts):
    return parts[0] if len(parts) == 1 else jnp.concatenate(parts, axis=1)


class Held:
    def __init__(self, source, target, arrived):
        self.target, self.copy, self.there = target, None, False
        self.copy = pltpu.make_async_copy(source, target, arrived)
        self.copy.start()

    def __call__(self):
        if not self.there:
            self.copy.wait()
            self.there = True
        return self.target


class Sent:
    def __init__(self, outs, held, left):
        self.outs, self.held, self.left, self.copies = outs, held, left, []

    def __getitem__(self, at):
        return self.held[at]

    def start(self, at, part=None):
        source, target = self.held[at], self.outs[at]
        if part is not None:
            source, target = source.at[part], target.at[part]
        copy = pltpu.make_async_copy(source, target, self.left.at[len(self.copies)])
        copy.start()
        self.copies.append(copy)

    def finish(self):
        for copy in self.copies:
            copy.wait()


def part_shape(shape, part):
    if part is None:
        return shape
    kept = []
    for size, index in zip(shape, part):
        if isinstance(index, slice):
            kept.append(len(range(*index.indices(size))))
        elif not isinstance(index, int):
            kept.append(index.size)
    return tuple(kept)


def run(body, name, scalars, operands, results, scratch, most_copies):
    arrays = [array for array, _ in operands]
    taken = [
        part_shape(array.shape, part([None] * 99, 0) if callable(part) else part)
        for array, part in operands
    ]
    n, k, m = len(scalars), len(arrays), len(results)

    def kernel(*refs):
        given, sources, outs = refs[:n], refs[n : n + k], refs[n + k : n + k + m]
        refs = refs[n + k + m :]
        targets, held, own, (arrived, left) = refs[:k], refs[k : k + m], refs[k + m : -2], refs[-2:]
        ready = []
        for at, (source, (_, part)) in enumerate(zip(sources, operands)):
            if callable(part):
                part = part(given, None)
            source = source if part is None else source.at[part]
            ready.append(Held(source, targets[at], arrived.at[at]))
        sent = Sent(outs, held, left)
        body(given, ready, sent, *own)
        sent.finish()

    return pl.pallas_call(
        kernel,
        in_specs=[pl.BlockSpec(memory_space=pltpu.SMEM)] * n + [pl.BlockSpec(memory_space=pl.ANY)] * k,
        out_specs=[pl.BlockSpec(memory_space=pl.ANY)] * m,
        out_shape=[jax.ShapeDtypeStruct(*result) for result in results],
        scratch_shapes=[pltpu.VMEM(shape, array.dtype) for shape, array in zip(taken, arrays)]
        + [pltpu.VMEM(*result) for result in results]
        + scratch
        + [pltpu.SemaphoreType.DMA((k,)), pltpu.SemaphoreType.DMA((most_copies,))],
        compiler_params=pltpu.CompilerParams(vmem_limit_bytes=VMEM_BYTES),
        cost_estimate=LIGHT,
        name=name,
    )(*scalars, *arrays)


def whole(arrays):
    return [(array, None) for array in arrays]


def weight_rows(seq_index, head_width, weights):
    width, count = weights[0].shape[0], len(weights)
    pairs = head_width // BLK
    first = jnp.reshape(seq_index * head_width, (1,)).astype(jnp.int32)

    def cols(scalars, dry):
        start = 0 if dry is not None else pl.multiple_of(scalars[0][0], BLK)
        return (slice(0, width), pl.ds(start, head_width))

    def body(_, ready, sent):
        rows = sent[0]
        for at in range(count):
            taken = ready[at]()
            for pair in range(pairs):
                base = (pair * count + at) * BLK
                rows[base : base + BLK, :] = taken[:, pair * BLK : (pair + 1) * BLK].T
        sent.start(0)

    operands = [(weight, cols) for weight in weights]
    return run(body, "weight_rows", [first], operands, [((count * head_width, width), BF)], [], 1)[0]


def out_rows_part(blocks, more, height, model):
    def part(scalars, dry):
        start = 0 if dry is not None else pl.multiple_of(scalars[0][blocks] + more, BLK)
        return (pl.ds(start, height), slice(0, model))

    return part


def project(plan, blocks, tokens, grads, rows, out_weight, scale):
    count, (step, model) = len(tokens), tokens[0].shape
    width = rows.shape[0] // 3
    pairs = width // BLK
    across, down = ((width, count * step), BF), ((count * step, width), BF)

    def body(_, ready, sent):
        rows, out_rows, far_rows = ready[0], ready[1], ready[2 : 2 + count]
        tokens_here, grads_here = ready[2 + count : 2 + 2 * count], ready[2 + 2 * count :]
        queries_t, out_grads_t, keys_t, values_t, keys, values = (sent[at] for at in range(6))
        own_grads = grads_here[0]()[...]
        for at in range(count):
            sent[6 + at][...] = dot(far_rows[at]()[...], own_grads, LAST_LAST).astype(BF)
            sent.start(6 + at)
        for at in range(2):
            sent[6 + count + at][...] = own_grads[at * step // 2 : (at + 1) * step // 2]
            sent.start(6 + count + at)
        for at in range(count):
            span = slice(at * step, (at + 1) * step)
            heads_t = dot(rows()[...], tokens_here[at]()[...], LAST_LAST)
            for pair in range(pairs):
                own = slice(pair * BLK, (pair + 1) * BLK)
                base = pair * 3 * BLK
                queries_t[own, span] = heads_t[base : base + BLK].astype(BF) * scale
                key_part = heads_t[base + BLK : base + 2 * BLK]
                value_part = heads_t[base + 2 * BLK : base + 3 * BLK]
                keys_t[own, span] = key_part.astype(BF)
                values_t[own, span] = value_part.astype(BF)
                keys[span, own] = key_part.T.astype(BF)
                values[span, own] = value_part.T.astype(BF)
        for at in (0, 2, 3, 4, 5):
            sent.start(at)
        for at in range(count):
            span = slice(at * step, (at + 1) * step)
            out_grads_t[:, span] = dot(out_rows()[...], grads_here[at]()[...], LAST_LAST).astype(BF)
        sent.start(1)

    operands = [(rows, None), (out_weight, out_rows_part(blocks, 0, width, model))]
    operands += [
        (out_weight, out_rows_part(blocks + 1 + at, 0, width, model)) for at in range(count)
    ]
    operands += whole(tokens) + whole(grads)
    results = [across] * 4 + [down] * 2 + [((width, step), BF)] * count
    results += [((step // 2, model), BF)] * 2
    return run(body, "project", [plan], operands, results, [], 8 + count)


def attend(
    place_of, offsets, head_base, places, queries_t, out_grads_t, key_refs, sums, put, slots, blocks, head_size
):
    keys_t, values_t, keys, values = key_refs
    key_at = lax.broadcasted_iota(jnp.int32, (BLK, BLK), 0)
    query_at = lax.broadcasted_iota(jnp.int32, (BLK, BLK), 1)
    causal = key_at <= query_at
    first_head = lax.broadcasted_iota(jnp.int32, (2 * head_size, BLK), 0) < head_size
    plus = functools.partial(functools.reduce, jnp.add)
    cut = [slice(slot * BLK, (slot + 1) * BLK) for slot in range(slots)]

    for step in range(queries_t.shape[1] // BLK):
        place = places + step
        block = place_of[place]
        cols = slice(step * BLK, (step + 1) * BLK)
        pair_queries = queries_t[:, cols]
        pair_grads = out_grads_t[:, cols]
        scored = []
        for half in range(2):
            head = head_base + half
            rows = slice(half * head_size, (half + 1) * head_size)
            keep = first_head if half == 0 else ~first_head
            head_queries = jnp.where(keep, pair_queries, jnp.zeros_like(pair_queries))
            head_grads = jnp.where(keep, pair_grads, jnp.zeros_like(pair_grads))
            named, usable = [], []
            for slot in range(slots):
                offset = offsets[(head * blocks + block) * slots + slot]
                usable.append(offset <= block)
                named.append(place_of[jnp.where(offset <= block, block - offset, 0)])
            spans = [pl.ds(pl.multiple_of(at * BLK, BLK), BLK) for at in named]
            seen_keys = jnp.concatenate([keys[span, :] for span in spans], axis=0)
            seen_values = jnp.concatenate([values[span, :] for span in spans], axis=0)
            scores = jnp.dot(seen_keys, head_queries, preferred_element_type=F32)
            prob_grad = jnp.dot(seen_values, head_grads, preferred_element_type=F32)
            scores = [
                jnp.where(causal if slot == 0 else usable[slot], scores[cut[slot]], -jnp.inf)
                for slot in range(slots)
            ]
            scored.append((rows, named, spans, scores, [prob_grad[part] for part in cut]))
        parts = []
        for rows, named, spans, scores, prob_grad in scored:
            top = jnp.max(functools.reduce(jnp.maximum, scores), axis=0, keepdims=True)
            raised = [jnp.exp(part - top) for part in scores]
            total = jnp.sum(plus(raised), axis=0, keepdims=True)
            inverse = 1.0 / total
            probs = [part * inverse for part in raised]
            probs_half = jnp.concatenate([part.astype(BF) for part in probs], axis=0)
            delta = jnp.sum(
                plus([part * grad for part, grad in zip(probs, prob_grad)]), axis=0, keepdims=True
            )
            score_grad = jnp.concatenate(
                [(part * (grad - delta)).astype(BF) for part, grad in zip(probs, prob_grad)], axis=0
            )
            seen_values_t = side_by_side([values_t[rows, span] for span in spans])
            seen_keys_t = side_by_side([keys_t[rows, span] for span in spans])
            attended = jnp.dot(seen_values_t, probs_half, preferred_element_type=F32)
            query_grad = jnp.dot(seen_keys_t, score_grad, preferred_element_type=F32)
            put(rows, cols, attended, query_grad * (1.0 / math.sqrt(head_size)))
            value_part = dot(out_grads_t[rows, cols], probs_half, LAST_LAST)
            key_part = dot(queries_t[rows, cols], score_grad, LAST_LAST)
            parts.append((rows, named, key_part, value_part))
        key_acc, value_acc = sums()
        for rows, named, key_part, value_part in parts:
            for at, part in zip(named, cut):
                key_acc[at, rows, :] += key_part[:, part]
                value_acc[at, rows, :] += value_part[:, part]


def own_half(plan, offsets, tokens, rows, projected):
    width, half = projected[0].shape
    heads, blocks, slots = offsets.shape
    head_size, pairs, total, count = width // heads, width // BLK, blocks * BLK, len(tokens)
    half_across, across, down = ((width, half), BF), ((width, total), BF), ((total, width), BF)
    sums = ((pairs, blocks, BLK, BLK), F32)
    scale = 1.0 / math.sqrt(head_size)

    def body(scalars, ready, sent):
        rows, tokens_here = ready[0], ready[1 : 1 + count]
        queries_t, out_grads_t, keys_in, values_in, keys_down, values_down = ready[1 + count :]
        later_queries_t, keys_t, values_t, keys, values = (sent[at] for at in range(5))
        attended_t, query_grad_t, key_acc, value_acc = (sent[at] for at in range(5, 9))
        key_acc[...] = jnp.zeros(key_acc.shape, F32)
        value_acc[...] = jnp.zeros(value_acc.shape, F32)
        step = tokens[0].shape[0]
        for at in range(count):
            span = slice(at * step, (at + 1) * step)
            placed = slice(half + at * step, half + (at + 1) * step)
            for pair in range(pairs):
                own = slice(pair * BLK, (pair + 1) * BLK)
                pair_rows = rows()[pair * 3 * BLK : (pair + 1) * 3 * BLK, :]
                heads_t = dot(pair_rows, tokens_here[at]()[...], LAST_LAST)
                later_queries_t[own, span] = heads_t[:BLK].astype(BF) * scale
                keys_t[own, placed] = heads_t[BLK : 2 * BLK].astype(BF)
                values_t[own, placed] = heads_t[2 * BLK :].astype(BF)
                keys[placed, own] = heads_t[BLK : 2 * BLK].T.astype(BF)
                values[placed, own] = heads_t[2 * BLK :].T.astype(BF)
        keys_t[:, :half] = keys_in()[...]
        values_t[:, :half] = values_in()[...]
        keys[:half, :] = keys_down()[...]
        values[:half, :] = values_down()[...]
        for at in range(5):
            sent.start(at)

        for pair in range(pairs):
            own = slice(pair * BLK, (pair + 1) * BLK)

            def put(at_rows, cols, attended, query_grad):
                placed = slice(own.start + at_rows.start, own.start + at_rows.stop)
                attended_t[placed, cols] = attended.astype(BF)
                query_grad_t[placed, cols] = query_grad.astype(BF)

            attend(
                scalars[0],
                scalars[1],
                2 * pair,
                0,
                queries_t().at[own, :],
                out_grads_t().at[own, :],
                (keys_t.at[own, :], values_t.at[own, :], keys.at[:, own], values.at[:, own]),
                lambda pair=pair: (key_acc.at[pair], value_acc.at[pair]),
                put,
                slots,
                blocks,
                head_size,
            )
            for at in (5, 6):
                sent.start(at, (own, slice(0, half)))
            for at in (7, 8):
                sent.start(at, (pair,))

    results = [half_across, across, across, down, down, half_across, half_across, sums, sums]
    operands = whole([rows, *tokens, *projected])
    return run(
        body, "own_half", [plan, offsets.reshape(-1)], operands, results, [], 5 + 4 * pairs
    )


def later_half(
    plan, offsets, order_at, far_grads_t, pair, first, tokens, grads, attended, before, rows
):
    width, half = first[0].shape
    heads, blocks, slots = offsets.shape
    head_size, total = width // heads, blocks * BLK
    near, step = len(far_grads_t), far_grads_t[0].shape[1]
    model, count = tokens[0].shape[1], len(tokens)
    own = slice(pair * BLK, (pair + 1) * BLK)
    across, half_across, down = (own, slice(0, total)), (own, slice(0, half)), (slice(0, total), own)
    last, final = bool(grads), rows is not None

    def body(scalars, ready, sent, out_grads_t, stay, leave):
        plan = scalars[0]
        queries_t, keys_t, values_t, keys, values = (part() for part in ready[near : near + 5])
        query_grad_first = ready[near + 7]
        tokens_here = ready[near + 8 : near + 8 + count]
        grads_here = ready[near + 8 + count : near + 8 + count + len(grads)]
        attended_here = ready[near + 8 + count + len(grads) :]
        attended_here, shares_here = attended_here[: len(attended)], attended_here[len(attended) :]
        attended_t = sent[0]
        for at in range(near):
            out_grads_t[:, at * step : (at + 1) * step] = ready[at]()[...]

        def columns(place, at):
            left = place // 2 * step + at
            return (leave if place % 2 else stay), slice(left, left + BLK)

        def put(at_rows, cols, attended, query_grad):
            attended_t[at_rows, cols] = attended.astype(BF)
            target, placed = columns(near + cols.start // step, cols.start % step)
            target[at_rows, placed] = query_grad.astype(BF)

        attend(
            plan,
            scalars[1],
            2 * pair,
            blocks // 2,
            queries_t,
            out_grads_t,
            (keys_t, values_t, keys, values),
            lambda: (ready[near + 5](), ready[near + 6]()),
            put,
            slots,
            blocks,
            head_size,
        )
        if not last:
            sent.start(0)
        for at in range(0, half, BLK):
            target, cols = columns(at // step, at % step)
            target[:BLK, cols] = query_grad_first()[:, at : at + BLK]
        key_acc, value_acc = ready[near + 5](), ready[near + 6]()
        for at in range(blocks):
            target, cols = columns(at * BLK // step, at * BLK % step)
            target[BLK : 2 * BLK, cols] = key_acc[at].astype(BF)
            target[2 * BLK :, cols] = value_acc[at].astype(BF)
        for at, held in ((1, stay), (2, leave)):
            for cols in range(0, half, BLK):
                sent[at][cols : cols + BLK, :] = held[:, cols : cols + BLK].T
            sent.start(at)
        if final:
            parts = [(sent[1], shares_here[-1], pair)]
            parts += [(shares_here[at], shares_here[-1], at) for at in range(len(before))]
            lefts = [left()[...] if isinstance(left, Held) else left[step:, :] for left, _, _ in parts]
            left = jnp.concatenate(lefts, axis=1)
            model_n = rows.shape[1]
            for col in range(0, model_n, 2 * BLK):
                cols = slice(col, col + 2 * BLK)
                held = [
                    right()[at * 3 * BLK : (at + 1) * 3 * BLK, cols] for _, right, at in parts
                ]
                sent[5][:, cols] = jnp.dot(
                    left, jnp.concatenate(held, axis=0), preferred_element_type=F32
                )
            sent.start(5)

        def put_terms(at, lefts, rights):
            pieces = [[part() for part in right] for right in rights]
            for col in range(0, model, 2 * BLK):
                spans = [
                    pl.ds(pl.multiple_of(plan[order_at + col // BLK + side] * BLK, BLK), BLK)
                    for side in range(2)
                ]
                terms = 0.0
                for left, right in zip(lefts, pieces):
                    cut = [side_by_side([part[:, span] for span in spans]) for part in right]
                    terms += jnp.dot(
                        left, jnp.concatenate(cut, axis=0), preferred_element_type=F32
                    )
                target, cols = sent[at + col // (model // 2)], col % (model // 2)
                target[:, cols : cols + 2 * BLK] = terms.astype(target.dtype)
                part = (slice(0, target.shape[0]), slice(cols, cols + 2 * BLK))
                sent.start(at + col // (model // 2), part)

        if last:
            lefts = [attended_here[0]()[...]]
            lefts.append(
                jnp.concatenate([part()[...] for part in attended_here[1:]] + [attended_t[...]], axis=0)
            )
            pieces = [[part() for part in grads_here[:near]], [part() for part in grads_here[near:]]]
            own_rows = plan[order_at + model // BLK + model // width]
            for at in range(model // width):
                span = pl.ds(
                    pl.multiple_of(plan[order_at + model // BLK + at] * width, width), width
                )
                terms = 0.0
                for left, right in zip(lefts, pieces):
                    taken = jnp.concatenate([part[:, span] for part in right], axis=0)
                    terms += jnp.dot(left, taken, preferred_element_type=F32)
                goes = jnp.where(own_rows == 0, terms[BLK:], terms[:BLK]).astype(BF)
                stays = jnp.where(own_rows == 0, terms[:BLK], terms[BLK:])
                cols = slice(at * BLK, (at + 1) * BLK)
                for side in range(width // BLK):
                    held = slice(side * BLK, (side + 1) * BLK)
                    sent[6][held, cols] = goes[:, held]
                    sent[7][held, cols] = stays[:, held]
            sent.start(6)
            sent.start(7)
        put_terms(3, [stay[...], leave[...]], [tokens_here[0::2], tokens_here[1::2]])

    (queries_t, keys_t, values_t, keys, values, _, query_grad_t, key_acc, value_acc) = first
    sums = (pair, slice(0, blocks), slice(0, BLK), slice(0, BLK))
    operands = [(part, (own, slice(0, step))) for part in far_grads_t]
    operands += [(queries_t, half_across), (keys_t, across), (values_t, across)]
    operands += [(keys, down), (values, down), (key_acc, sums), (value_acc, sums)]
    operands += [(query_grad_t, half_across)]
    operands += whole([*tokens, *grads, *attended])
    results = [((BLK, half), BF)] + [((half, 3 * BLK), BF)] * 2
    results += [((3 * BLK, model // 2), BF), ((3 * BLK, model // 2), F32)]
    if final:
        results += [((half - step, model), F32)]
        far_places = (slice(step, half), slice(0, 3 * BLK))
        operands += [(part, far_places) for part in before]
        operands += [(rows, None)]
    if last:
        results += [((width, model // 2), BF), ((width, model // 2), F32)]
    scratch = [pltpu.VMEM((BLK, half), BF)] + [pltpu.VMEM((3 * BLK, half), BF)] * 2
    return run(body, "later_half", [plan, offsets.reshape(-1)], operands, results, scratch, 6 + model // (2 * BLK))


def halves(pieces, low):
    kept = {place: part for place, part in pieces.items() if (place // low) % 2 == 0}
    return side_by_side([pieces[place + low].astype(BF) for place in kept]), kept


def joined(kept, came):
    block = came.shape[1] // len(kept)
    return {
        place: part + came[:, at * block : (at + 1) * block].astype(F32)
        for at, (place, part) in enumerate(kept.items())
    }


def tied(values, others):
    return list(lax.optimization_barrier((*values, *others))[: len(values)])


def phase(*values):
    flat, tree = jax.tree.flatten(values)
    return jax.tree.unflatten(tree, lax.optimization_barrier(tuple(flat)))


def to_owner(block_sum):
    seq_count, batch_count = lax.axis_size("seq"), lax.axis_size("batch")
    ratio = batch_count // seq_count
    moves = [
        (s * batch_count + b, (b // ratio) * batch_count + s * ratio + b % ratio)
        for s in range(seq_count)
        for b in range(batch_count)
    ]
    return lax.ppermute(block_sum, ("seq", "batch"), moves)


def per_device(hidden, grad_out, block_offsets, w_query, w_key, w_value, w_out):
    tokens = hidden[0]
    grad_rows = grad_out[0]
    offsets = block_offsets[0]
    row_count, width = tokens.shape
    seq_count = lax.axis_size("seq")
    batch_count = lax.axis_size("batch")
    seq_at = lax.axis_index("seq")
    head_width = width // seq_count
    head_size = head_width // offsets.shape[0]
    pairs = head_width // BLK
    half_count = seq_count // 2

    weights = (w_query, w_key, w_value)
    rows = weight_rows(seq_at, head_width, weights)
    shard_blocks = row_count // BLK
    blocks = shard_blocks * seq_count
    block_at = jnp.arange(blocks, dtype=jnp.int32)
    place_of = ((block_at // shard_blocks) ^ seq_at) * shard_blocks + block_at % shard_blocks
    col_block = width // batch_count
    direct = col_block == BLK
    col_order = jnp.arange(width // BLK, dtype=jnp.int32)
    if direct:
        half_at = jnp.arange(batch_count // 2, dtype=jnp.int32) * 2
        col_order = lax.axis_index("batch") ^ jnp.concatenate([half_at + 1, half_at])
    seq_rows = (seq_at ^ jnp.asarray([0, *range(half_count, seq_count)])) * head_width
    batch_at = lax.axis_index("batch")
    ratio = batch_count // seq_count
    out_order = jnp.concatenate(
        [(batch_at // ratio) ^ jnp.arange(seq_count), jnp.reshape(batch_at % ratio, (1,))]
    )
    plan = jnp.concatenate([place_of, seq_rows, col_order, out_order])
    order_at = blocks + 1 + half_count
    plan = plan.astype(jnp.int32)

    mate_rows = weight_rows(seq_at ^ 1, head_width, weights)
    near_tokens = spread(tokens, "seq", half_count)
    near_grads = spread(grad_rows, "seq", half_count)
    projected = project(
        plan, blocks, near_tokens, near_grads, rows, w_out, 1.0 / math.sqrt(head_size)
    )
    projected, far_grads_t, (early, late) = projected[:6], projected[6:-2], projected[-2:]
    far_tokens = swap(tokens, "seq", half_count)
    plan, flat_offsets = plan, offsets.reshape(-1)
    far_tokens, mate_rows, projected, far_grads_t, early, late, plan, flat_offsets = phase(
        far_tokens, mate_rows, projected, far_grads_t, early, late, plan, flat_offsets
    )
    offsets = flat_offsets.reshape(offsets.shape)
    far_grads_t = [swap(part, "seq", half_count + at) for at, part in enumerate(far_grads_t)]
    early = swap(early, "seq", half_count)
    far_tokens = spread(far_tokens, "seq", half_count)
    first = own_half(plan, offsets, far_tokens, rows, projected)
    first, far_grads_t, early, late = phase(first, far_grads_t, early, late)
    late = swap(late, "seq", half_count)
    early = spread(early, "seq", half_count)
    all_tokens = near_tokens + far_tokens

    even = range(0, batch_count, 2)

    def begin(sent_terms, kept_terms):
        if direct:
            return sent_terms, {p: kept_terms[:, p // 2 * BLK : (p // 2 + 1) * BLK] for p in even}
        terms = jnp.concatenate([sent_terms.astype(F32), kept_terms], axis=1)
        pieces = [
            lax.dynamic_slice(
                terms, (0, (batch_at ^ p) * col_block), (terms.shape[0], col_block)
            )
            for p in range(batch_count)
        ]
        return side_by_side([pieces[p + 1].astype(BF) for p in even]), {p: pieces[p] for p in even}

    def begin_out(attended, terms):
        if direct and ratio == pairs:
            return begin(*terms)
        attended_t = jnp.concatenate([first[5], jnp.concatenate(attended, axis=0)], axis=1)
        grads = jnp.concatenate(all_grads, axis=0)
        terms = jnp.dot(attended_t, grads, preferred_element_type=F32)
        height = head_width // ratio
        pieces = []
        for p in range(batch_count):
            target = batch_at ^ p
            corner = ((target % ratio) * height, (target // ratio) * head_width)
            pieces.append(lax.dynamic_slice(terms, corner, (height, head_width)))
        return side_by_side([pieces[p + 1].astype(BF) for p in even]), {p: pieces[p] for p in even}

    kept, came_terms, stayed, came, attended = [], [], [], [], []
    for pair in range(pairs):
        last = pair == pairs - 1
        all_grads = []
        if last:
            late = spread(late, "seq", half_count)
            all_grads = near_grads + [part for both in zip(early, late) for part in both]
        far_attended, stay, leave, *terms = later_half(
            plan,
            offsets,
            order_at,
            far_grads_t,
            pair,
            first,
            all_tokens,
            all_grads if direct and ratio == pairs else [],
            [first[5], *attended] if last and direct and ratio == pairs else [],
            stayed,
            rows if last else None,
        )
        if last:
            stay, leave, terms, came_terms, came = phase(stay, leave, terms, came_terms, came)
        else:
            stay, leave, terms, far_attended, early, late, first = phase(
                stay, leave, terms, far_attended, early, late, first
            )
        attended.append(far_attended)
        stayed.append(stay)
        came.append(swap(leave, "seq", 1))
        if not last:
            goes, kept_head = begin(*terms)
            kept.append(kept_head)
            came_terms.append(swap(goes, "batch", 1))

    levels = [1 << bit for bit in range(1, batch_count.bit_length() - 1)]
    goes, kept_out = begin_out(attended, terms[3:])
    came_out = swap(goes, "batch", 1)
    goes_head, kept_head = begin(*terms[:2])
    pieces = [None] * len(kept)
    lags = []

    def start(at, turn):
        goes, kept = halves(pieces[at], levels[turn - lags[at]])
        return at, kept, swap(goes, "batch", levels[turn - lags[at]])

    def due(turn):
        return [at for at in range(len(pieces)) if 0 <= turn - lags[at] < len(levels)]

    moving = []

    held = [rows, mate_rows]
    sent = []
    for at in range(1, half_count):
        total = terms[2][(at - 1) * row_count : at * row_count]
        for pair in range(pairs):
            mate = came[pair][at * row_count : (at + 1) * row_count]
            weight = mate_rows[pair * 3 * BLK : (pair + 1) * 3 * BLK]
            total += jnp.dot(mate, weight, preferred_element_type=F32)
        sent.append(total.astype(BF))
    cut = row_count // 2
    sent = [(part[:cut], part[cut:]) for part in sent]
    stayed, came, sent_after = phase(stayed, came, sent)
    partial = 0.0
    for pair in range(pairs):
        for side, parts in enumerate((stayed, came)):
            weight = held[side][pair * 3 * BLK : (pair + 1) * 3 * BLK]
            partial += jnp.dot(parts[pair][:row_count], weight, preferred_element_type=F32)
    token_parts = [swap(part[0], "seq", 2 * at) for at, part in enumerate(sent, 1)]
    came_head = swap(goes_head, "batch", 1)

    merged = direct and ratio == pairs
    turn, out_at = 0, 0 if merged else pairs - 1
    while turn < 2 + len(levels):
        transfers = [came for _, _, came in moving]
        if turn == 0:
            came_terms, came_out, sent_after = phase(came_terms, came_out, sent_after)
            pieces = [joined(*both) for both in zip(kept, came_terms)]
            pieces.append(joined(kept_out, came_out))
            if merged:
                pieces = [{p: jnp.concatenate([part[p] for part in pieces], axis=0) for p in even}]
            later_parts = [swap(part[1], "seq", 2 * at) for at, part in enumerate(sent_after, 1)]
            lags = [1] * len(pieces)
        elif turn == 1:
            transfers, came_head, token_parts = phase(transfers, came_head, token_parts)
            pieces.append(joined(kept_head, came_head))
            lags.append(2)
        elif turn == 2:
            transfers, later_parts = phase(transfers, later_parts)
        else:
            transfers = phase(transfers)[0]
        for (at, kept_now, _), came_now in zip(moving, transfers):
            pieces[at] = joined(kept_now, came_now)
        turn += 1
        moving = [start(at, turn) for at in due(turn)]
        if turn == 1 + len(levels):
            out_sum, head_sums = pieces[out_at][0], []
            if merged:
                top = 3 * BLK * (pairs - 1)
                head_sums = [out_sum[at : at + 3 * BLK] for at in range(0, top, 3 * BLK)]
                out_sum = side_by_side(
                    [out_sum[at : at + BLK] for at in range(top, top + head_width, BLK)]
                )
            out_part = to_owner(out_sum)[None]

    grad_hidden = partial
    for both in zip(token_parts, later_parts):
        grad_hidden = grad_hidden + jnp.concatenate(both, axis=0).astype(F32)
    grad_hidden = grad_hidden.astype(BF)
    head_sums += [pieces[at][0] for at in range(len(pieces)) if at != out_at]
    row_block = width // batch_count
    head_part = jnp.stack([part.reshape(3, BLK, row_block) for part in head_sums], axis=1)
    head_part = head_part.reshape(3, head_width, row_block).transpose(0, 2, 1)
    grad_weights = jnp.concatenate([head_part, out_part], axis=0)
    norm_factor = 1.0 / math.sqrt(row_count * seq_count * batch_count)
    return (grad_hidden[None], grad_weights * norm_factor)


def solution(mesh):
    placed = (
        P("batch", "seq", None),
        P("batch", "seq", None),
        P("batch", "seq", None, None),
        P(),
        P(),
        P(),
        P(),
    )
    return jax.shard_map(
        per_device,
        mesh=mesh,
        in_specs=placed,
        out_specs=(P("batch", "seq", None), P(None, "batch", "seq")),
        check_vma=False,
    )
```

```python
import functools
import math

import jax
import jax.numpy as jnp
from jax import lax
from jax.experimental import pallas as pl
from jax.experimental.pallas import tpu as pltpu
from jax.sharding import PartitionSpec as P

BLK = 128
BF = jnp.bfloat16
F32 = jnp.float32
LAST_LAST = (((1,), (1,)), ((), ()))
VMEM_BYTES = 66584576
LIGHT = pl.CostEstimate(flops=1, bytes_accessed=1, transcendentals=0)


def dot(left_side, right_side, dims):
    return lax.dot_general(left_side, right_side, dims, preferred_element_type=F32)


def swap(value, axis, distance):
    count = lax.axis_size(axis)
    return lax.ppermute(value, axis, [(at, at ^ distance) for at in range(count)])


def spread(shard, axis, count):
    pieces = {0: shard}
    bit = count // 2
    while bit:
        for place in sorted(pieces):
            pieces[place | bit] = swap(pieces[place], axis, bit)
        bit //= 2
    return [pieces[place] for place in sorted(pieces)]


def side_by_side(parts):
    return parts[0] if len(parts) == 1 else jnp.concatenate(parts, axis=1)


class Held:
    def __init__(self, source, target, arrived):
        self.target, self.copy, self.there = target, None, False
        self.copy = pltpu.make_async_copy(source, target, arrived)
        self.copy.start()

    def __call__(self):
        if not self.there:
            self.copy.wait()
            self.there = True
        return self.target


class Sent:
    def __init__(self, outs, held, left):
        self.outs, self.held, self.left, self.copies = outs, held, left, []

    def __getitem__(self, at):
        return self.held[at]

    def start(self, at, part=None):
        source, target = self.held[at], self.outs[at]
        if part is not None:
            source, target = source.at[part], target.at[part]
        copy = pltpu.make_async_copy(source, target, self.left.at[len(self.copies)])
        copy.start()
        self.copies.append(copy)

    def finish(self):
        for copy in self.copies:
            copy.wait()


def part_shape(shape, part):
    if part is None:
        return shape
    kept = []
    for size, index in zip(shape, part):
        if isinstance(index, slice):
            kept.append(len(range(*index.indices(size))))
        elif not isinstance(index, int):
            kept.append(index.size)
    return tuple(kept)


def run(body, name, scalars, operands, results, scratch, most_copies):
    arrays = [array for array, _ in operands]
    taken = [
        part_shape(array.shape, part([None] * 99, 0) if callable(part) else part)
        for array, part in operands
    ]
    n, k, m = len(scalars), len(arrays), len(results)

    def kernel(*refs):
        given, sources, outs = refs[:n], refs[n : n + k], refs[n + k : n + k + m]
        refs = refs[n + k + m :]
        targets, held, own, (arrived, left) = refs[:k], refs[k : k + m], refs[k + m : -2], refs[-2:]
        ready = []
        for at, (source, (_, part)) in enumerate(zip(sources, operands)):
            if callable(part):
                part = part(given, None)
            source = source if part is None else source.at[part]
            ready.append(Held(source, targets[at], arrived.at[at]))
        sent = Sent(outs, held, left)
        body(given, ready, sent, *own)
        sent.finish()

    return pl.pallas_call(
        kernel,
        in_specs=[pl.BlockSpec(memory_space=pltpu.SMEM)] * n + [pl.BlockSpec(memory_space=pl.ANY)] * k,
        out_specs=[pl.BlockSpec(memory_space=pl.ANY)] * m,
        out_shape=[jax.ShapeDtypeStruct(*result) for result in results],
        scratch_shapes=[pltpu.VMEM(shape, array.dtype) for shape, array in zip(taken, arrays)]
        + [pltpu.VMEM(*result) for result in results]
        + scratch
        + [pltpu.SemaphoreType.DMA((k,)), pltpu.SemaphoreType.DMA((most_copies,))],
        compiler_params=pltpu.CompilerParams(vmem_limit_bytes=VMEM_BYTES),
        cost_estimate=LIGHT,
        name=name,
    )(*scalars, *arrays)


def whole(arrays):
    return [(array, None) for array in arrays]


def weight_rows(seq_index, head_width, weights):
    width, count = weights[0].shape[0], len(weights)
    pairs = head_width // BLK
    first = jnp.reshape(seq_index * head_width, (1,)).astype(jnp.int32)

    def cols(scalars, dry):
        start = 0 if dry is not None else pl.multiple_of(scalars[0][0], BLK)
        return (slice(0, width), pl.ds(start, head_width))

    def body(_, ready, sent):
        rows = sent[0]
        for at in range(count):
            taken = ready[at]()
            for pair in range(pairs):
                base = (pair * count + at) * BLK
                rows[base : base + BLK, :] = taken[:, pair * BLK : (pair + 1) * BLK].T
        sent.start(0)

    operands = [(weight, cols) for weight in weights]
    return run(body, "weight_rows", [first], operands, [((count * head_width, width), BF)], [], 1)[0]


def out_rows_part(blocks, more, height, model):
    def part(scalars, dry):
        start = 0 if dry is not None else pl.multiple_of(scalars[0][blocks] + more, BLK)
        return (pl.ds(start, height), slice(0, model))

    return part


def project(plan, blocks, tokens, grads, rows, out_weight, scale):
    count, (step, model) = len(tokens), tokens[0].shape
    width = rows.shape[0] // 3
    pairs = width // BLK
    across, down = ((width, count * step), BF), ((count * step, width), BF)

    def body(_, ready, sent):
        rows, out_rows, far_rows = ready[0], ready[1], ready[2 : 2 + count]
        tokens_here, grads_here = ready[2 + count : 2 + 2 * count], ready[2 + 2 * count :]
        queries_t, out_grads_t, keys_t, values_t, keys, values = (sent[at] for at in range(6))
        own_grads = grads_here[0]()[...]
        for at in range(count):
            sent[6 + at][...] = dot(far_rows[at]()[...], own_grads, LAST_LAST).astype(BF)
            sent.start(6 + at)
        for at in range(2):
            sent[6 + count + at][...] = own_grads[at * step // 2 : (at + 1) * step // 2]
            sent.start(6 + count + at)
        for at in range(count):
            span = slice(at * step, (at + 1) * step)
            heads_t = dot(rows()[...], tokens_here[at]()[...], LAST_LAST)
            for pair in range(pairs):
                own = slice(pair * BLK, (pair + 1) * BLK)
                base = pair * 3 * BLK
                queries_t[own, span] = heads_t[base : base + BLK].astype(BF) * scale
                key_part = heads_t[base + BLK : base + 2 * BLK]
                value_part = heads_t[base + 2 * BLK : base + 3 * BLK]
                keys_t[own, span] = key_part.astype(BF)
                values_t[own, span] = value_part.astype(BF)
                keys[span, own] = key_part.T.astype(BF)
                values[span, own] = value_part.T.astype(BF)
        for at in (0, 2, 3, 4, 5):
            sent.start(at)
        for at in range(count):
            span = slice(at * step, (at + 1) * step)
            out_grads_t[:, span] = dot(out_rows()[...], grads_here[at]()[...], LAST_LAST).astype(BF)
        sent.start(1)

    operands = [(rows, None), (out_weight, out_rows_part(blocks, 0, width, model))]
    operands += [
        (out_weight, out_rows_part(blocks + 1 + at, 0, width, model)) for at in range(count)
    ]
    operands += whole(tokens) + whole(grads)
    results = [across] * 4 + [down] * 2 + [((width, step), BF)] * count
    results += [((step // 2, model), BF)] * 2
    return run(body, "project", [plan], operands, results, [], 8 + count)


def attend(
    place_of, offsets, head_base, places, queries_t, out_grads_t, key_refs, sums, put, slots, blocks, head_size
):
    keys_t, values_t, keys, values = key_refs
    key_at = lax.broadcasted_iota(jnp.int32, (BLK, BLK), 0)
    query_at = lax.broadcasted_iota(jnp.int32, (BLK, BLK), 1)
    causal = key_at <= query_at
    first_head = lax.broadcasted_iota(jnp.int32, (2 * head_size, BLK), 0) < head_size
    plus = functools.partial(functools.reduce, jnp.add)
    cut = [slice(slot * BLK, (slot + 1) * BLK) for slot in range(slots)]

    for step in range(queries_t.shape[1] // BLK):
        place = places + step
        block = place_of[place]
        cols = slice(step * BLK, (step + 1) * BLK)
        pair_queries = queries_t[:, cols]
        pair_grads = out_grads_t[:, cols]
        scored = []
        for half in range(2):
            head = head_base + half
            rows = slice(half * head_size, (half + 1) * head_size)
            keep = first_head if half == 0 else ~first_head
            head_queries = jnp.where(keep, pair_queries, jnp.zeros_like(pair_queries))
            head_grads = jnp.where(keep, pair_grads, jnp.zeros_like(pair_grads))
            named, usable = [], []
            for slot in range(slots):
                offset = offsets[(head * blocks + block) * slots + slot]
                usable.append(offset <= block)
                named.append(place_of[jnp.where(offset <= block, block - offset, 0)])
            spans = [pl.ds(pl.multiple_of(at * BLK, BLK), BLK) for at in named]
            seen_keys = jnp.concatenate([keys[span, :] for span in spans], axis=0)
            seen_values = jnp.concatenate([values[span, :] for span in spans], axis=0)
            scores = jnp.dot(seen_keys, head_queries, preferred_element_type=F32)
            prob_grad = jnp.dot(seen_values, head_grads, preferred_element_type=F32)
            scores = [
                jnp.where(causal if slot == 0 else usable[slot], scores[cut[slot]], -jnp.inf)
                for slot in range(slots)
            ]
            scored.append((rows, named, spans, scores, [prob_grad[part] for part in cut]))
        parts = []
        for rows, named, spans, scores, prob_grad in scored:
            top = jnp.max(functools.reduce(jnp.maximum, scores), axis=0, keepdims=True)
            raised = [jnp.exp(part - top) for part in scores]
            total = jnp.sum(plus(raised), axis=0, keepdims=True)
            inverse = 1.0 / total
            probs = [part * inverse for part in raised]
            probs_half = jnp.concatenate([part.astype(BF) for part in probs], axis=0)
            delta = jnp.sum(
                plus([part * grad for part, grad in zip(probs, prob_grad)]), axis=0, keepdims=True
            )
            score_grad = jnp.concatenate(
                [(part * (grad - delta)).astype(BF) for part, grad in zip(probs, prob_grad)], axis=0
            )
            seen_values_t = side_by_side([values_t[rows, span] for span in spans])
            seen_keys_t = side_by_side([keys_t[rows, span] for span in spans])
            attended = jnp.dot(seen_values_t, probs_half, preferred_element_type=F32)
            query_grad = jnp.dot(seen_keys_t, score_grad, preferred_element_type=F32)
            put(rows, cols, attended, query_grad * (1.0 / math.sqrt(head_size)))
            value_part = dot(out_grads_t[rows, cols], probs_half, LAST_LAST)
            key_part = dot(queries_t[rows, cols], score_grad, LAST_LAST)
            parts.append((rows, named, key_part, value_part))
        key_acc, value_acc = sums()
        for rows, named, key_part, value_part in parts:
            for at, part in zip(named, cut):
                key_acc[at, rows, :] += key_part[:, part]
                value_acc[at, rows, :] += value_part[:, part]


def own_half(plan, offsets, tokens, rows, projected):
    width, half = projected[0].shape
    heads, blocks, slots = offsets.shape
    head_size, pairs, total, count = width // heads, width // BLK, blocks * BLK, len(tokens)
    half_across, across, down = ((width, half), BF), ((width, total), BF), ((total, width), BF)
    sums = ((pairs, blocks, BLK, BLK), F32)
    scale = 1.0 / math.sqrt(head_size)

    def body(scalars, ready, sent):
        rows, tokens_here = ready[0], ready[1 : 1 + count]
        queries_t, out_grads_t, keys_in, values_in, keys_down, values_down = ready[1 + count :]
        later_queries_t, keys_t, values_t, keys, values = (sent[at] for at in range(5))
        attended_t, query_grad_t, key_acc, value_acc = (sent[at] for at in range(5, 9))
        key_acc[...] = jnp.zeros(key_acc.shape, F32)
        value_acc[...] = jnp.zeros(value_acc.shape, F32)
        step = tokens[0].shape[0]
        for at in range(count):
            span = slice(at * step, (at + 1) * step)
            placed = slice(half + at * step, half + (at + 1) * step)
            for pair in range(pairs):
                own = slice(pair * BLK, (pair + 1) * BLK)
                pair_rows = rows()[pair * 3 * BLK : (pair + 1) * 3 * BLK, :]
                heads_t = dot(pair_rows, tokens_here[at]()[...], LAST_LAST)
                later_queries_t[own, span] = heads_t[:BLK].astype(BF) * scale
                keys_t[own, placed] = heads_t[BLK : 2 * BLK].astype(BF)
                values_t[own, placed] = heads_t[2 * BLK :].astype(BF)
                keys[placed, own] = heads_t[BLK : 2 * BLK].T.astype(BF)
                values[placed, own] = heads_t[2 * BLK :].T.astype(BF)
        keys_t[:, :half] = keys_in()[...]
        values_t[:, :half] = values_in()[...]
        keys[:half, :] = keys_down()[...]
        values[:half, :] = values_down()[...]
        for at in range(5):
            sent.start(at)

        for pair in range(pairs):
            own = slice(pair * BLK, (pair + 1) * BLK)

            def put(at_rows, cols, attended, query_grad):
                placed = slice(own.start + at_rows.start, own.start + at_rows.stop)
                attended_t[placed, cols] = attended.astype(BF)
                query_grad_t[placed, cols] = query_grad.astype(BF)

            attend(
                scalars[0],
                scalars[1],
                2 * pair,
                0,
                queries_t().at[own, :],
                out_grads_t().at[own, :],
                (keys_t.at[own, :], values_t.at[own, :], keys.at[:, own], values.at[:, own]),
                lambda pair=pair: (key_acc.at[pair], value_acc.at[pair]),
                put,
                slots,
                blocks,
                head_size,
            )
            for at in (5, 6):
                sent.start(at, (own, slice(0, half)))
            for at in (7, 8):
                sent.start(at, (pair,))

    results = [half_across, across, across, down, down, half_across, half_across, sums, sums]
    operands = whole([rows, *tokens, *projected])
    return run(
        body, "own_half", [plan, offsets.reshape(-1)], operands, results, [], 5 + 4 * pairs
    )


def later_half(
    plan, offsets, order_at, far_grads_t, pair, first, tokens, grads, attended, before, rows
):
    width, half = first[0].shape
    heads, blocks, slots = offsets.shape
    head_size, total = width // heads, blocks * BLK
    near, step = len(far_grads_t), far_grads_t[0].shape[1]
    model, count = tokens[0].shape[1], len(tokens)
    own = slice(pair * BLK, (pair + 1) * BLK)
    across, half_across, down = (own, slice(0, total)), (own, slice(0, half)), (slice(0, total), own)
    last, final = bool(grads), rows is not None

    def body(scalars, ready, sent, out_grads_t, stay, leave):
        plan = scalars[0]
        queries_t, keys_t, values_t, keys, values = (part() for part in ready[near : near + 5])
        query_grad_first = ready[near + 7]
        tokens_here = ready[near + 8 : near + 8 + count]
        grads_here = ready[near + 8 + count : near + 8 + count + len(grads)]
        attended_here = ready[near + 8 + count + len(grads) :]
        attended_here, shares_here = attended_here[: len(attended)], attended_here[len(attended) :]
        attended_t = sent[0]
        for at in range(near):
            out_grads_t[:, at * step : (at + 1) * step] = ready[at]()[...]

        def columns(place, at):
            left = place // 2 * step + at
            return (leave if place % 2 else stay), slice(left, left + BLK)

        def put(at_rows, cols, attended, query_grad):
            attended_t[at_rows, cols] = attended.astype(BF)
            target, placed = columns(near + cols.start // step, cols.start % step)
            target[at_rows, placed] = query_grad.astype(BF)

        attend(
            plan,
            scalars[1],
            2 * pair,
            blocks // 2,
            queries_t,
            out_grads_t,
            (keys_t, values_t, keys, values),
            lambda: (ready[near + 5](), ready[near + 6]()),
            put,
            slots,
            blocks,
            head_size,
        )
        if not last:
            sent.start(0)
        for at in range(0, half, BLK):
            target, cols = columns(at // step, at % step)
            target[:BLK, cols] = query_grad_first()[:, at : at + BLK]
        key_acc, value_acc = ready[near + 5](), ready[near + 6]()
        for at in range(blocks):
            target, cols = columns(at * BLK // step, at * BLK % step)
            target[BLK : 2 * BLK, cols] = key_acc[at].astype(BF)
            target[2 * BLK :, cols] = value_acc[at].astype(BF)
        for at, held in ((1, stay), (2, leave)):
            for cols in range(0, half, BLK):
                sent[at][cols : cols + BLK, :] = held[:, cols : cols + BLK].T
            sent.start(at)
        if final:
            parts = [(sent[1], shares_here[-1], pair)]
            parts += [(shares_here[at], shares_here[-1], at) for at in range(len(before))]
            lefts = [left()[...] if isinstance(left, Held) else left[step:, :] for left, _, _ in parts]
            left = jnp.concatenate(lefts, axis=1)
            model_n = rows.shape[1]
            for col in range(0, model_n, 2 * BLK):
                cols = slice(col, col + 2 * BLK)
                held = [
                    right()[at * 3 * BLK : (at + 1) * 3 * BLK, cols] for _, right, at in parts
                ]
                sent[5][:, cols] = jnp.dot(
                    left, jnp.concatenate(held, axis=0), preferred_element_type=F32
                )
            sent.start(5)

        def put_terms(at, lefts, rights):
            pieces = [[part() for part in right] for right in rights]
            for col in range(0, model, 2 * BLK):
                spans = [
                    pl.ds(pl.multiple_of(plan[order_at + col // BLK + side] * BLK, BLK), BLK)
                    for side in range(2)
                ]
                terms = 0.0
                for left, right in zip(lefts, pieces):
                    cut = [side_by_side([part[:, span] for span in spans]) for part in right]
                    terms += jnp.dot(
                        left, jnp.concatenate(cut, axis=0), preferred_element_type=F32
                    )
                target, cols = sent[at + col // (model // 2)], col % (model // 2)
                target[:, cols : cols + 2 * BLK] = terms.astype(target.dtype)
                part = (slice(0, target.shape[0]), slice(cols, cols + 2 * BLK))
                sent.start(at + col // (model // 2), part)

        if last:
            lefts = [attended_here[0]()[...]]
            lefts.append(
                jnp.concatenate([part()[...] for part in attended_here[1:]] + [attended_t[...]], axis=0)
            )
            pieces = [[part() for part in grads_here[:near]], [part() for part in grads_here[near:]]]
            own_rows = plan[order_at + model // BLK + model // width]
            for at in range(model // width):
                span = pl.ds(
                    pl.multiple_of(plan[order_at + model // BLK + at] * width, width), width
                )
                terms = 0.0
                for left, right in zip(lefts, pieces):
                    taken = jnp.concatenate([part[:, span] for part in right], axis=0)
                    terms += jnp.dot(left, taken, preferred_element_type=F32)
                goes = jnp.where(own_rows == 0, terms[BLK:], terms[:BLK]).astype(BF)
                stays = jnp.where(own_rows == 0, terms[:BLK], terms[BLK:])
                cols = slice(at * BLK, (at + 1) * BLK)
                for side in range(width // BLK):
                    held = slice(side * BLK, (side + 1) * BLK)
                    sent[6][held, cols] = goes[:, held]
                    sent[7][held, cols] = stays[:, held]
            sent.start(6)
            sent.start(7)
        put_terms(3, [stay[...], leave[...]], [tokens_here[0::2], tokens_here[1::2]])

    (queries_t, keys_t, values_t, keys, values, _, query_grad_t, key_acc, value_acc) = first
    sums = (pair, slice(0, blocks), slice(0, BLK), slice(0, BLK))
    operands = [(part, (own, slice(0, step))) for part in far_grads_t]
    operands += [(queries_t, half_across), (keys_t, across), (values_t, across)]
    operands += [(keys, down), (values, down), (key_acc, sums), (value_acc, sums)]
    operands += [(query_grad_t, half_across)]
    operands += whole([*tokens, *grads, *attended])
    results = [((BLK, half), BF)] + [((half, 3 * BLK), BF)] * 2
    results += [((3 * BLK, model // 2), BF), ((3 * BLK, model // 2), F32)]
    if final:
        results += [((half - step, model), F32)]
        far_places = (slice(step, half), slice(0, 3 * BLK))
        operands += [(part, far_places) for part in before]
        operands += [(rows, None)]
    if last:
        results += [((width, model // 2), BF), ((width, model // 2), F32)]
    scratch = [pltpu.VMEM((BLK, half), BF)] + [pltpu.VMEM((3 * BLK, half), BF)] * 2
    return run(body, "later_half", [plan, offsets.reshape(-1)], operands, results, scratch, 6 + model // (2 * BLK))


def halves(pieces, low):
    kept = {place: part for place, part in pieces.items() if (place // low) % 2 == 0}
    return side_by_side([pieces[place + low].astype(BF) for place in kept]), kept


def joined(kept, came):
    block = came.shape[1] // len(kept)
    return {
        place: part + came[:, at * block : (at + 1) * block].astype(F32)
        for at, (place, part) in enumerate(kept.items())
    }


def tied(values, others):
    return list(lax.optimization_barrier((*values, *others))[: len(values)])


def phase(*values):
    flat, tree = jax.tree.flatten(values)
    return jax.tree.unflatten(tree, lax.optimization_barrier(tuple(flat)))


def to_owner(block_sum):
    seq_count, batch_count = lax.axis_size("seq"), lax.axis_size("batch")
    ratio = batch_count // seq_count
    moves = [
        (s * batch_count + b, (b // ratio) * batch_count + s * ratio + b % ratio)
        for s in range(seq_count)
        for b in range(batch_count)
    ]
    return lax.ppermute(block_sum, ("seq", "batch"), moves)


def per_device(hidden, grad_out, block_offsets, w_query, w_key, w_value, w_out):
    tokens = hidden[0]
    grad_rows = grad_out[0]
    offsets = block_offsets[0]
    row_count, width = tokens.shape
    seq_count = lax.axis_size("seq")
    batch_count = lax.axis_size("batch")
    seq_at = lax.axis_index("seq")
    head_width = width // seq_count
    head_size = head_width // offsets.shape[0]
    pairs = head_width // BLK
    half_count = seq_count // 2

    weights = (w_query, w_key, w_value)
    rows = weight_rows(seq_at, head_width, weights)
    shard_blocks = row_count // BLK
    blocks = shard_blocks * seq_count
    block_at = jnp.arange(blocks, dtype=jnp.int32)
    place_of = ((block_at // shard_blocks) ^ seq_at) * shard_blocks + block_at % shard_blocks
    col_block = width // batch_count
    direct = col_block == BLK
    col_order = jnp.arange(width // BLK, dtype=jnp.int32)
    if direct:
        half_at = jnp.arange(batch_count // 2, dtype=jnp.int32) * 2
        col_order = lax.axis_index("batch") ^ jnp.concatenate([half_at + 1, half_at])
    seq_rows = (seq_at ^ jnp.asarray([0, *range(half_count, seq_count)])) * head_width
    batch_at = lax.axis_index("batch")
    ratio = batch_count // seq_count
    out_order = jnp.concatenate(
        [(batch_at // ratio) ^ jnp.arange(seq_count), jnp.reshape(batch_at % ratio, (1,))]
    )
    plan = jnp.concatenate([place_of, seq_rows, col_order, out_order])
    order_at = blocks + 1 + half_count
    plan = plan.astype(jnp.int32)

    mate_rows = weight_rows(seq_at ^ 1, head_width, weights)
    near_tokens = spread(tokens, "seq", half_count)
    near_grads = spread(grad_rows, "seq", half_count)
    projected = project(
        plan, blocks, near_tokens, near_grads, rows, w_out, 1.0 / math.sqrt(head_size)
    )
    projected, far_grads_t, (early, late) = projected[:6], projected[6:-2], projected[-2:]
    far_tokens = swap(tokens, "seq", half_count)
    plan, flat_offsets = plan, offsets.reshape(-1)
    far_tokens, mate_rows, projected, far_grads_t, early, late, plan, flat_offsets = phase(
        far_tokens, mate_rows, projected, far_grads_t, early, late, plan, flat_offsets
    )
    offsets = flat_offsets.reshape(offsets.shape)
    far_grads_t = [swap(part, "seq", half_count + at) for at, part in enumerate(far_grads_t)]
    early = swap(early, "seq", half_count)
    far_tokens = spread(far_tokens, "seq", half_count)
    first = own_half(plan, offsets, far_tokens, rows, projected)
    first, far_grads_t, early, late = phase(first, far_grads_t, early, late)
    late = swap(late, "seq", half_count)
    early = spread(early, "seq", half_count)
    all_tokens = near_tokens + far_tokens

    even = range(0, batch_count, 2)

    def begin(sent_terms, kept_terms):
        if direct:
            return sent_terms, {p: kept_terms[:, p // 2 * BLK : (p // 2 + 1) * BLK] for p in even}
        terms = jnp.concatenate([sent_terms.astype(F32), kept_terms], axis=1)
        pieces = [
            lax.dynamic_slice(
                terms, (0, (batch_at ^ p) * col_block), (terms.shape[0], col_block)
            )
            for p in range(batch_count)
        ]
        return side_by_side([pieces[p + 1].astype(BF) for p in even]), {p: pieces[p] for p in even}

    def begin_out(attended, terms):
        if direct and ratio == pairs:
            return begin(*terms)
        attended_t = jnp.concatenate([first[5], jnp.concatenate(attended, axis=0)], axis=1)
        grads = jnp.concatenate(all_grads, axis=0)
        terms = jnp.dot(attended_t, grads, preferred_element_type=F32)
        height = head_width // ratio
        pieces = []
        for p in range(batch_count):
            target = batch_at ^ p
            corner = ((target % ratio) * height, (target // ratio) * head_width)
            pieces.append(lax.dynamic_slice(terms, corner, (height, head_width)))
        return side_by_side([pieces[p + 1].astype(BF) for p in even]), {p: pieces[p] for p in even}

    kept, came_terms, stayed, came, attended = [], [], [], [], []
    for pair in range(pairs):
        last = pair == pairs - 1
        all_grads = []
        if last:
            late = spread(late, "seq", half_count)
            all_grads = near_grads + [part for both in zip(early, late) for part in both]
        far_attended, stay, leave, *terms = later_half(
            plan,
            offsets,
            order_at,
            far_grads_t,
            pair,
            first,
            all_tokens,
            all_grads if direct and ratio == pairs else [],
            [first[5], *attended] if last and direct and ratio == pairs else [],
            stayed,
            rows if last else None,
        )
        if last:
            stay, leave, terms, came_terms, came = phase(stay, leave, terms, came_terms, came)
        else:
            stay, leave, terms, far_attended, early, late, first = phase(
                stay, leave, terms, far_attended, early, late, first
            )
        attended.append(far_attended)
        stayed.append(stay)
        came.append(swap(leave, "seq", 1))
        if not last:
            goes, kept_head = begin(*terms)
            kept.append(kept_head)
            came_terms.append(swap(goes, "batch", 1))

    levels = [1 << bit for bit in range(1, batch_count.bit_length() - 1)]
    goes, kept_out = begin_out(attended, terms[3:])
    came_out = swap(goes, "batch", 1)
    goes_head, kept_head = begin(*terms[:2])
    pieces = [None] * len(kept)
    lags = []

    def start(at, turn):
        goes, kept = halves(pieces[at], levels[turn - lags[at]])
        return at, kept, swap(goes, "batch", levels[turn - lags[at]])

    def due(turn):
        return [at for at in range(len(pieces)) if 0 <= turn - lags[at] < len(levels)]

    moving = []

    held = [rows, mate_rows]
    sent = []
    for at in range(1, half_count):
        total = terms[2][(at - 1) * row_count : at * row_count]
        for pair in range(pairs):
            mate = came[pair][at * row_count : (at + 1) * row_count]
            weight = mate_rows[pair * 3 * BLK : (pair + 1) * 3 * BLK]
            total += jnp.dot(mate, weight, preferred_element_type=F32)
        sent.append(total.astype(BF))
    cut = row_count // 2
    sent = [(part[:cut], part[cut:]) for part in sent]
    stayed, came, sent_after = phase(stayed, came, sent)
    partial = 0.0
    for pair in range(pairs):
        for side, parts in enumerate((stayed, came)):
            weight = held[side][pair * 3 * BLK : (pair + 1) * 3 * BLK]
            partial += jnp.dot(parts[pair][:row_count], weight, preferred_element_type=F32)
    token_parts = [swap(part[0], "seq", 2 * at) for at, part in enumerate(sent, 1)]
    came_head = swap(goes_head, "batch", 1)

    merged = direct and ratio == pairs
    turn, out_at = 0, 0 if merged else pairs - 1
    while turn < 2 + len(levels):
        transfers = [came for _, _, came in moving]
        if turn == 0:
            came_terms, came_out, sent_after = phase(came_terms, came_out, sent_after)
            pieces = [joined(*both) for both in zip(kept, came_terms)]
            pieces.append(joined(kept_out, came_out))
            if merged:
                pieces = [{p: jnp.concatenate([part[p] for part in pieces], axis=0) for p in even}]
            later_parts = [swap(part[1], "seq", 2 * at) for at, part in enumerate(sent_after, 1)]
            lags = [1] * len(pieces)
        elif turn == 1:
            transfers, came_head, token_parts = phase(transfers, came_head, token_parts)
            pieces.append(joined(kept_head, came_head))
            lags.append(2)
        elif turn == 2:
            transfers, later_parts = phase(transfers, later_parts)
        else:
            transfers = phase(transfers)[0]
        for (at, kept_now, _), came_now in zip(moving, transfers):
            pieces[at] = joined(kept_now, came_now)
        turn += 1
        moving = [start(at, turn) for at in due(turn)]
        if turn == 1 + len(levels):
            out_sum, head_sums = pieces[out_at][0], []
            if merged:
                top = 3 * BLK * (pairs - 1)
                head_sums = [out_sum[at : at + 3 * BLK] for at in range(0, top, 3 * BLK)]
                out_sum = side_by_side(
                    [out_sum[at : at + BLK] for at in range(top, top + head_width, BLK)]
                )
            out_part = to_owner(out_sum.astype(BF)).astype(F32)[None]

    grad_hidden = partial
    for both in zip(token_parts, later_parts):
        grad_hidden = grad_hidden + jnp.concatenate(both, axis=0).astype(F32)
    grad_hidden = grad_hidden.astype(BF)
    head_sums += [pieces[at][0] for at in range(len(pieces)) if at != out_at]
    row_block = width // batch_count
    head_part = jnp.stack([part.reshape(3, BLK, row_block) for part in head_sums], axis=1)
    head_part = head_part.reshape(3, head_width, row_block).transpose(0, 2, 1)
    grad_weights = jnp.concatenate([head_part, out_part], axis=0)
    norm_factor = 1.0 / math.sqrt(row_count * seq_count * batch_count)
    return (grad_hidden[None], grad_weights * norm_factor)


def solution(mesh):
    placed = (
        P("batch", "seq", None),
        P("batch", "seq", None),
        P("batch", "seq", None, None),
        P(),
        P(),
        P(),
        P(),
    )
    return jax.shard_map(
        per_device,
        mesh=mesh,
        in_specs=placed,
        out_specs=(P("batch", "seq", None), P(None, "batch", "seq")),
        check_vma=False,
    )
```
